256 devices in a mesh: pairs: 8 (over y, core), proj: 32 (over x, z).
Axes of the slice: x: 4, y: 4, z: 8, core: 2. Of those that a mesh axis runs over, the one named last changes fastest.
Arguments:
- q_fact: bfloat16 [98304, 32], P(('pairs', 'proj')), parts along dimension 0, may hold values from -6 to 6
- p_fact: bfloat16 [147456, 32], P(('pairs', 'proj')), parts along dimension 0, may hold values from -6 to 6
- q_cot: bfloat16 [98304, 2048], P(('pairs', 'proj')), parts along dimension 0, may hold values from -0.796875 to 0.796875
- p_cot: bfloat16 [147456, 2048], P(('pairs', 'proj')), parts along dimension 0, may hold values from -0.796875 to 0.796875
- passage_of: int32 [3072], P('pairs'), parts along dimension 0, may hold values from 0 to 383, each once
- projection: bfloat16 [32768, 4096], P('proj'), may hold values from -0.03125 to 0.03125
Outputs:
- features: float32 [3072, 4096], P(('pairs', 'proj')), parts along dimension 0
The draws below stay inside these ranges and needn't reach their ends.
There are 8 independent parts, one for each index of `pairs`. The reference program is written for one: setup_inputs(seed, part) draws one part's arguments, and reference() takes and returns one part's arrays. A program takes and returns all parts, laid end to end along the dimension named above; an argument that names none is the same for every part. Nothing has to cross between parts.
Inputs may be any that keep to these rules, and one draw needn't show every extreme that they name: `passage_of`: each passage belongs to exactly one pair.
All inputs are finite; a program needn't handle non-finite values.
Results may differ from the reference program's by a relative error of at most 0.01.
Values may be sent and summed in bfloat16 or wider, within the bound.
No kernel may reach another device: no remote copies, remote signals or barrier semaphores. Data moves between devices by JAX's collectives and lax.ppermute only.
A program may use at most 64 MiB of HBM per device.

```python
import jax
import jax.numpy as jnp

KV = 1024
R = 16
LAYERS = 2
K = 4096
QLEN = 32
PLEN = 48
G = 32768
PAIRS = 384


def shard_levels(stream_key, shape, split, least, largest):
    gain = 1.0
    for position, parts in split:
        draws = jax.random.uniform(jax.random.fold_in(jax.random.fold_in(stream_key, 6), position), (parts,), jnp.float32, least / len(split), largest / len(split))
        gain = gain * jnp.repeat(jnp.exp(draws), shape[position] // parts).reshape((-1,) + (1,) * (len(shape) - 1 - position))
    return gain


def gaussian(rng, extent, scale, most, cuts=(), held_as=jnp.bfloat16):
    drawn = jax.random.normal(rng, extent, jnp.float32) * scale
    if len(cuts) > 0:
        drawn = shard_levels(rng, extent, cuts, -0.22, 0.18) * drawn
    return jnp.clip(drawn, min=-most, max=most).astype(held_as)


def setup_inputs(seed: int = 0, part: int = 0) -> dict:
    seeds = jax.random.split(jax.random.key(seed), 7)
    part_splits = jax.random.split(jax.random.fold_in(seeds[6], part), 7)
    q_fact = gaussian(part_splits[0], (PAIRS * QLEN, LAYERS * R), 1.0, 6.0, ((0, 32),))
    p_fact = gaussian(part_splits[1], (PAIRS * PLEN, LAYERS * R), 1.0, 6.0, ((0, 32),))
    q_cot = gaussian(part_splits[2], (PAIRS * QLEN, LAYERS * KV), 0.1, 0.796875, ((0, 32),))
    p_cot = gaussian(part_splits[3], (PAIRS * PLEN, LAYERS * KV), 0.1, 0.796875, ((0, 32),))
    passage_of = jax.random.permutation(part_splits[4], PAIRS).astype(jnp.int32)
    projection = gaussian(seeds[5], (G, K), G ** -0.5, 0.03125, ((0, 32),))
    return dict(q_fact=q_fact, p_fact=p_fact, q_cot=q_cot, p_cot=p_cot, passage_of=passage_of, projection=projection)


def seq_grads(cot, fact, length):
    cot4 = cot.astype(jnp.float32).reshape(-1, length, LAYERS, KV)
    fact4 = fact.astype(jnp.float32).reshape(-1, length, LAYERS, R)
    grads = jnp.einsum("stla,stlr->slar", cot4, fact4)
    return grads.reshape(grads.shape[0], -1).astype(jnp.bfloat16)


def reference(q_fact, p_fact, q_cot, p_cot, passage_of, projection):
    q_grad = seq_grads(q_cot, q_fact, QLEN)
    p_grad = seq_grads(p_cot, p_fact, PLEN)
    picked = jnp.take(p_grad, passage_of.astype(jnp.int32), axis=0)
    pair_grad = (q_grad.astype(jnp.float32) + picked.astype(jnp.float32)).astype(jnp.bfloat16)
    return jnp.dot(pair_grad, projection, preferred_element_type=jnp.float32)
```

```python
import jax
import jax.numpy as jnp
from jax import lax
from jax.experimental import pallas as pl
from jax.experimental.pallas import tpu as pltpu
from jax.sharding import Mesh, PartitionSpec as P

KV = 1024
R = 16
QLEN = 32
PLEN = 48
K = 4096
NX, NZ = 4, 8
N = NX * NZ
MINE = 12
PAIRS = N * MINE
ROWS = MINE * 8
VMEM = 60 * 1024 * 1024
BF = jnp.bfloat16
F32 = jnp.float32


def iota(shape, dim):
    return lax.broadcasted_iota(jnp.int32, shape, dim)


def dot(a, b):
    return lax.dot_general(a, b, (((1,), (0,)), ((), ())), preferred_element_type=F32)


def grads_kernel(qf, pf, qc, pc, out):
    layer = pl.program_id(0)
    lane = iota((ROWS, 128), 1)
    for kind, (fact, cot, length) in enumerate(((qf, qc, QLEN), (pf, pc, PLEN))):
        tokens = MINE * length
        row = iota((2 * ROWS, 2 * R), 0)
        rank = jnp.where(row >= ROWS, 8, 0) + (row & 7) + layer * R
        pick = jnp.where(iota((2 * ROWS, 2 * R), 1) == rank, 1.0, 0.0).astype(BF)
        row = iota((2 * ROWS, tokens), 0)
        item = jnp.where(row >= ROWS, row - ROWS, row) >> 3
        token = iota((2 * ROWS, tokens), 1) - item * length
        spread = jnp.where((token >= 0) & (token < length), dot(pick, fact[...]), 0.0)
        grad = dot(spread.astype(BF), cot[...])
        for j in range(8):
            top = grad[:ROWS, 128 * j : 128 * j + 128]
            low = grad[ROWS:, 128 * j : 128 * j + 128]
            even = jnp.where(lane < 64, top, pltpu.roll(low, 64, 1))
            odd = jnp.where(lane < 64, pltpu.roll(top, 64, 1), low)
            out[2 * j, kind * ROWS : kind * ROWS + ROWS, :] = even.astype(BF)
            out[2 * j + 1, kind * ROWS : kind * ROWS + ROWS, :] = odd.astype(BF)


def grads(q_fact, p_fact, q_cot, p_cot):
    return pl.pallas_call(
        grads_kernel,
        grid=(2,),
        in_specs=[
            pl.BlockSpec((2 * R, MINE * QLEN), lambda l: (0, 0)),
            pl.BlockSpec((2 * R, MINE * PLEN), lambda l: (0, 0)),
            pl.BlockSpec((MINE * QLEN, KV), lambda l: (0, l)),
            pl.BlockSpec((MINE * PLEN, KV), lambda l: (0, l)),
        ],
        out_specs=pl.BlockSpec((N // 2, 2 * ROWS, 128), lambda l: (l, 0, 0)),
        out_shape=jax.ShapeDtypeStruct((N, 2 * ROWS, 128), BF),
        compiler_params=pltpu.CompilerParams(vmem_limit_bytes=VMEM),
        cost_estimate=pl.CostEstimate(flops=800_000_000, bytes_accessed=5_500_000, transcendentals=0),
    )(q_fact.T, p_fact.T, q_cot, p_cot)


def product_kernel(recv, passage, order, proj, out, wide_q, wide_p, pair):
    @pl.when(pl.program_id(0) == 0)
    def _():
        r, c = iota((256, 256), 0), iota((256, 256), 1)
        swap = jnp.where(c == (r & 31) * 8 + (r >> 5), 1.0, 0.0).astype(BF)
        for g in range(PAIRS // 32):
            parts = []
            for kind in range(2):
                pieces, at, need = [], g * 256, 256
                while need:
                    src, off = at // ROWS, at % ROWS
                    take = min(ROWS - off, need)
                    pieces.append(recv[src, kind * ROWS + off : kind * ROWS + off + take, :])
                    at, need = at + take, need - take
                parts.append(jnp.concatenate(pieces, axis=0))
            mixed = dot(swap, jnp.concatenate(parts, axis=1)).astype(BF)
            for b in range(8):
                wide_q[32 * g : 32 * g + 32, 128 * b : 128 * b + 128] = mixed[32 * b : 32 * b + 32, :128]
                wide_p[32 * g : 32 * g + 32, 128 * b : 128 * b + 128] = mixed[32 * b : 32 * b + 32, 128:]
        hot = jnp.where(iota((PAIRS, PAIRS), 0) == passage[...], 1.0, 0.0).astype(BF)
        picked = lax.dot_general(hot, wide_p[...], (((0,), (0,)), ((), ())), preferred_element_type=F32)
        summed = (wide_q[...].astype(F32) + picked).astype(BF)
        pair[...] = dot(summed, order[...]).astype(BF)

    out[...] = dot(pair[...], proj[...]).astype(BF)


def product(recv, passage_of, projection):
    u, v = iota((1024, 1024), 0), iota((1024, 1024), 1)
    order = jnp.where(v == (u & 63) * 16 + ((u >> 6) & 1) * 8 + (u >> 7), 1.0, 0.0).astype(BF)
    tile = 512
    return pl.pallas_call(
        product_kernel,
        grid=(K // tile,),
        in_specs=[
            pl.BlockSpec((N, 2 * ROWS, 128), lambda n: (0, 0, 0)),
            pl.BlockSpec((1, PAIRS), lambda n: (0, 0)),
            pl.BlockSpec((1024, 1024), lambda n: (0, 0)),
            pl.BlockSpec((1024, tile), lambda n: (0, n)),
        ],
        out_specs=pl.BlockSpec((PAIRS, tile), lambda n: (0, n)),
        out_shape=jax.ShapeDtypeStruct((PAIRS, K), BF),
        scratch_shapes=[pltpu.VMEM((PAIRS, 1024), BF)] * 3,
        compiler_params=pltpu.CompilerParams(vmem_limit_bytes=VMEM),
        cost_estimate=pl.CostEstimate(flops=5_000_000_000, bytes_accessed=15_000_000, transcendentals=0),
    )(recv, passage_of.reshape(1, PAIRS), order, projection)


def first_sum_kernel(part, out):
    total = part[0].astype(F32)
    for i in range(1, NX):
        total = total + part[i].astype(F32)
    total = total.astype(BF)
    stacked = jnp.concatenate([total[:, KV * q : KV * q + KV] for q in range(4)], axis=0)
    r, c = iota((4 * ROWS, 4 * ROWS), 0), iota((4 * ROWS, 4 * ROWS), 1)
    hot = jnp.zeros((4 * ROWS, 4 * ROWS), F32)
    z = r // 48
    quarter = (r - z * 48) // MINE
    item = r - z * 48 - quarter * MINE
    hot = jnp.where(c == quarter * ROWS + z * MINE + item, 1.0, 0.0).astype(BF)
    out[...] = dot(hot, stacked).astype(BF).reshape(NZ, 48, KV)


def first_sum(part):
    return pl.pallas_call(
        first_sum_kernel,
        out_shape=jax.ShapeDtypeStruct((NZ, 48, KV), BF),
        compiler_params=pltpu.CompilerParams(vmem_limit_bytes=VMEM),
        cost_estimate=pl.CostEstimate(flops=300_000_000, bytes_accessed=4_000_000, transcendentals=0),
    )(part)


def last_sum_kernel(part, out):
    total = part[0].astype(F32)
    for i in range(1, NZ):
        total = total + part[i].astype(F32)
    for q in range(4):
        out[:, KV * q : KV * q + KV] = total[MINE * q : MINE * q + MINE, :]


def last_sum(part):
    return pl.pallas_call(
        last_sum_kernel,
        out_shape=jax.ShapeDtypeStruct((MINE, K), F32),
        compiler_params=pltpu.CompilerParams(vmem_limit_bytes=VMEM),
        cost_estimate=pl.CostEstimate(flops=1_000_000, bytes_accessed=1_000_000, transcendentals=0),
    )(part)


def local(q_fact, p_fact, q_cot, p_cot, passage_of, projection):
    sent = grads(q_fact, p_fact, q_cot, p_cot)
    recv = lax.all_to_all(sent, ("px", "pz"), 0, 0, tiled=True)
    part = product(recv, passage_of, projection).reshape(NX, ROWS, K)
    part = lax.all_to_all(part, "px", 0, 0, tiled=True)
    part = first_sum(part)
    part = lax.all_to_all(part, "pz", 0, 0, tiled=True)
    return last_sum(part)


def solution(mesh):
    cut = Mesh(mesh.devices.reshape(mesh.shape["pairs"], NX, NZ), ("pairs", "px", "pz"))
    rows = P(("pairs", "px", "pz"), None)
    return jax.shard_map(
        local,
        mesh=cut,
        in_specs=(rows, rows, rows, rows, P("pairs"), P(("px", "pz"), None)),
        out_specs=rows,
        check_vma=False,
    )
```

```python
import jax
import jax.numpy as jnp
from jax import lax
from jax.experimental import pallas as pl
from jax.experimental.pallas import tpu as pltpu
from jax.sharding import Mesh, PartitionSpec as P

KV = 1024
R = 16
QLEN = 32
PLEN = 48
K = 4096
NX, NZ = 4, 8
N = NX * NZ
MINE = 12
PAIRS = N * MINE
G = 1024
ROWS = MINE * 8
VMEM = 40 * 1024 * 1024
BF = jnp.bfloat16
F32 = jnp.float32
ANY = pl.BlockSpec(memory_space=pl.ANY)
WHOLE = pl.BlockSpec(memory_space=pltpu.VMEM)


def iota(shape, dim):
    return lax.broadcasted_iota(jnp.int32, shape, dim)


def dot(a, b):
    return lax.dot_general(a, b, (((1,), (0,)), ((), ())), preferred_element_type=F32)


def ones_where(mask):
    return jnp.where(mask, 1.0, 0.0).astype(BF)


def call(kernel, out_shape, flops, moved, **kwargs):
    return pl.pallas_call(
        kernel,
        out_shape=out_shape,
        compiler_params=pltpu.CompilerParams(vmem_limit_bytes=VMEM),
        cost_estimate=pl.CostEstimate(flops=flops, bytes_accessed=moved, transcendentals=0),
        **kwargs,
    )


def array(*shape, dtype=BF):
    return jax.ShapeDtypeStruct(shape, dtype)


def grads(fact, cot, length):
    tokens = MINE * length

    def kernel(fact, cot, out):
        layer = pl.program_id(0)
        row = iota((2 * ROWS, 2 * R), 0)
        rank = jnp.where(row >= ROWS, 8, 0) + (row & 7) + layer * R
        pick = ones_where(iota((2 * ROWS, 2 * R), 1) == rank)
        row = iota((2 * ROWS, tokens), 0)
        item = jnp.where(row >= ROWS, row - ROWS, row) >> 3
        token = iota((2 * ROWS, tokens), 1) - item * length
        spread = jnp.where((token >= 0) & (token < length), dot(pick, fact[...]), 0.0)
        grad = dot(spread.astype(BF), cot[...])
        lane = iota((ROWS, 128), 1)
        for j in range(8):
            top = grad[:ROWS, 128 * j : 128 * j + 128]
            low = grad[ROWS:, 128 * j : 128 * j + 128]
            out[2 * j] = jnp.where(lane < 64, top, pltpu.roll(low, 64, 1)).astype(BF)
            out[2 * j + 1] = jnp.where(lane < 64, pltpu.roll(top, 64, 1), low).astype(BF)

    return call(
        kernel,
        array(N, ROWS, 128),
        400_000_000,
        3_000_000,
        grid=(2,),
        in_specs=[
            pl.BlockSpec((2 * R, tokens), lambda l: (0, 0)),
            pl.BlockSpec((tokens, KV), lambda l: (0, l)),
        ],
        out_specs=pl.BlockSpec((N // 2, ROWS, 128), lambda l: (l, 0, 0)),
    )(fact.T, cot)


def permuted(projection):
    def kernel(proj, out, order):
        @pl.when(pl.program_id(0) == 0)
        def _():
            u, v = iota((G, G), 0), iota((G, G), 1)
            order[...] = ones_where(v == (u & 63) * 16 + ((u >> 6) & 1) * 8 + (u >> 7))

        out[...] = dot(order[...], proj[...]).astype(BF)

    tile = pl.BlockSpec((G, 512), lambda n: (0, n))
    return call(
        kernel,
        array(G, K),
        2 * G * G * K,
        16_000_000,
        grid=(K // 512,),
        in_specs=[tile],
        out_specs=tile,
        scratch_shapes=[pltpu.VMEM((G, G), BF)],
    )(projection)


def widen(recv, out, rotated):
    r, c = iota((256, 256), 0), iota((256, 256), 1)
    swap = ones_where(c == (r & 31) * 8 + (r >> 5))
    x = lax.axis_index("px")
    for g in range(PAIRS // 32):
        mixed = dot(swap, recv[256 * g : 256 * g + 256, :]).astype(BF)
        if rotated:
            at = pl.multiple_of(((g // 3 - x) & 3) * ROWS + (g % 3) * 32, 32)
        else:
            at = 32 * g
        for b in range(8):
            out[pl.ds(at, 32), 128 * b : 128 * b + 128] = mixed[32 * b : 32 * b + 32, :]


def selected(recv, passage_of):
    def kernel(recv, passage, out, wide):
        widen(recv, wide, False)
        hot = ones_where(iota((PAIRS, PAIRS), 0) == passage[...])
        picked = lax.dot_general(hot, wide[...], (((0,), (0,)), ((), ())), preferred_element_type=F32)
        picked = picked.astype(BF)
        x = lax.axis_index("px")
        for i in range(NX):
            at = pl.multiple_of(((i - x) & 3) * ROWS, 32)
            out[pl.ds(at, ROWS), :] = picked[ROWS * i : ROWS * i + ROWS, :]

    return call(
        kernel,
        array(PAIRS, G),
        700_000_000,
        1_600_000,
        scratch_shapes=[pltpu.VMEM((PAIRS, G), BF)],
    )(recv.reshape(N * ROWS, 128), passage_of.reshape(1, PAIRS))


def quarters(pair, proj, outs):
    for half in range(2):
        part = dot(pair[...], proj[:, KV * half : KV * half + KV]).astype(BF)
        for d in range(NX):
            outs[4 * half + d][...] = part[ROWS * d : ROWS * d + ROWS, :]


def product_first(recv, picked, proj):
    def kernel(recv, picked, proj, pair, *rest):
        outs, (wide, held, sem) = rest[:8], rest[8:]
        copy = pltpu.make_async_copy(proj.at[:, : K // 2], held, sem)
        copy.start()
        widen(recv, wide, True)
        pair[...] = (wide[...].astype(F32) + picked[...].astype(F32)).astype(BF)
        copy.wait()
        quarters(pair, held, outs)

    return call(
        kernel,
        [array(PAIRS, G)] + [array(ROWS, KV)] * 8,
        2_500_000_000,
        8_000_000,
        in_specs=[WHOLE, WHOLE, ANY],
        scratch_shapes=[pltpu.VMEM((PAIRS, G), BF), pltpu.VMEM((G, K // 2), BF), pltpu.SemaphoreType.DMA],
    )(recv.reshape(N * ROWS, 128), picked, proj)


def product_second(pair, proj):
    def kernel(pair, proj, *outs):
        quarters(pair, proj, outs)

    return call(
        kernel,
        [array(ROWS, KV)] * 8,
        1_700_000_000,
        7_000_000,
        grid=(1,),
        in_specs=[pl.BlockSpec((PAIRS, G), lambda i: (0, 0)), pl.BlockSpec((G, K // 2), lambda i: (0, 1))],
        out_specs=[pl.BlockSpec((ROWS, KV), lambda i: (0, 0))] * 8,
    )(pair, proj)


def add(a, b):
    return (a.astype(F32) + b.astype(F32)).astype(BF)


def across_x(blocks):
    l0, l1, l2, l3, r0, r1, r2, r3 = blocks
    up = [(i, (i + 1) % NX) for i in range(NX)]
    down = [(i, (i - 1) % NX) for i in range(NX)]
    far_l = lax.ppermute(l2, "px", up)
    far_r = lax.ppermute(r2, "px", down)
    got_r = lax.ppermute(r1, "px", up)
    got_l = lax.ppermute(l3, "px", down)
    sum_l = lax.ppermute(add(l1, far_l), "px", up)
    sum_r = lax.ppermute(add(r3, far_r), "px", down)
    return (l0, got_l, sum_l, r0, got_r, sum_r)


def spread_z(terms):
    def kernel(l0, l1, l2, r0, r1, r2, out):
        left = (l0[...].astype(F32) + l1[...].astype(F32) + l2[...].astype(F32)).astype(BF)
        right = (r0[...].astype(F32) + r1[...].astype(F32) + r2[...].astype(F32)).astype(BF)
        stacked = jnp.concatenate([left[:, :512], left[:, 512:], right[:, :512], right[:, 512:]], axis=0)
        r, c = iota((4 * ROWS, 4 * ROWS), 0), iota((4 * ROWS, 4 * ROWS), 1)
        z = r // 48
        quarter = (r - z * 48) // MINE
        item = r - z * 48 - quarter * MINE
        hot = ones_where(c == quarter * ROWS + z * MINE + item)
        out[...] = dot(hot, stacked).astype(BF).reshape(NZ, 48, 512)

    part = call(kernel, array(NZ, 48, 512), 150_000_000, 2_000_000)(*terms)
    return lax.all_to_all(part, "pz", 0, 0, tiled=True)


def last_sum(first, second):
    def kernel(first, second, out):
        for half, part in enumerate((first, second)):
            total = part[0].astype(F32)
            for i in range(1, NZ):
                total = total + part[i].astype(F32)
            for q in range(4):
                at = 2048 * half + 512 * q
                out[:, at : at + 512] = total[MINE * q : MINE * q + MINE, :]

    return call(kernel, array(MINE, K, dtype=F32), 1_000_000, 1_000_000)(first, second)


def local(q_fact, p_fact, q_cot, p_cot, passage_of, projection):
    axes = ("px", "pz")
    p_recv = lax.all_to_all(grads(p_fact, p_cot, PLEN), axes, 0, 0, tiled=True)
    q_recv = lax.all_to_all(grads(q_fact, q_cot, QLEN), axes, 0, 0, tiled=True)
    proj = permuted(projection)
    picked = selected(p_recv, passage_of)
    pair, *first = product_first(q_recv, picked, proj)
    first = spread_z(across_x(first))
    second = spread_z(across_x(product_second(pair, proj)))
    return last_sum(first, second)


def solution(mesh):
    cut = Mesh(mesh.devices.reshape(mesh.shape["pairs"], NX, NZ), ("pairs", "px", "pz"))
    rows = P(("pairs", "px", "pz"), None)
    return jax.shard_map(
        local,
        mesh=cut,
        in_specs=(rows, rows, rows, rows, P("pairs"), P(("px", "pz"), None)),
        out_specs=rows,
        check_vma=False,
    )
```

```python
import jax
import jax.numpy as jnp
from jax import lax
from jax.experimental import pallas as pl
from jax.experimental.pallas import tpu as pltpu
from jax.sharding import Mesh, PartitionSpec as P

KV = 1024
R = 16
QLEN = 32
PLEN = 48
K = 4096
NX, NZ = 4, 8
N = NX * NZ
MINE = 12
PAIRS = N * MINE
G = 1024
ROWS = MINE * 8
MIB = 1024 * 1024
BF = jnp.bfloat16
F32 = jnp.float32
HBM = pl.BlockSpec(memory_space=pltpu.HBM)
WHOLE = pl.BlockSpec(memory_space=pltpu.VMEM)


def iota(shape, dim):
    return lax.broadcasted_iota(jnp.int32, shape, dim)


def dot(a, b):
    return lax.dot_general(a, b, (((1,), (0,)), ((), ())), preferred_element_type=F32)


def ones_where(mask):
    return jnp.where(mask, 1.0, 0.0).astype(BF)


def call(kernel, out_shape, flops, moved, vmem=24, **kwargs):
    return pl.pallas_call(
        kernel,
        out_shape=out_shape,
        compiler_params=pltpu.CompilerParams(vmem_limit_bytes=vmem * MIB),
        cost_estimate=pl.CostEstimate(flops=flops, bytes_accessed=moved, transcendentals=0),
        **kwargs,
    )


def array(*shape, dtype=BF):
    return jax.ShapeDtypeStruct(shape, dtype)


def grads(q_fact, p_fact, q_cot, p_cot):
    steps = 4
    cols = 2 * KV // steps

    def kernel(q_fact, p_fact, q_cot, p_cot, out, q_spread, p_spread):
        step = pl.program_id(0)
        lane = iota((ROWS, 128), 1)
        for kind, (fact, cot, length, spread) in enumerate(
            ((q_fact, q_cot, QLEN, q_spread), (p_fact, p_cot, PLEN, p_spread))
        ):
            tokens = MINE * length

            @pl.when(step % (steps // 2) == 0)
            def _():
                row = iota((2 * ROWS, 2 * R), 0)
                rank = jnp.where(row >= ROWS, 8, 0) + (row & 7) + (step // (steps // 2)) * R
                pick = ones_where(iota((2 * ROWS, 2 * R), 1) == rank)
                row = iota((2 * ROWS, tokens), 0)
                item = jnp.where(row >= ROWS, row - ROWS, row) >> 3
                token = iota((2 * ROWS, tokens), 1) - item * length
                held = (token >= 0) & (token < length)
                spread[...] = jnp.where(held, dot(pick, fact[...]), 0.0).astype(BF)

            grad = dot(spread[...], cot[...])
            for j in range(cols // 128):
                top = grad[:ROWS, 128 * j : 128 * j + 128]
                low = grad[ROWS:, 128 * j : 128 * j + 128]
                at = pl.ds(kind * ROWS, ROWS)
                out[2 * j, at, :] = jnp.where(lane < 64, top, pltpu.roll(low, 64, 1)).astype(BF)
                out[2 * j + 1, at, :] = jnp.where(lane < 64, pltpu.roll(top, 64, 1), low).astype(BF)

    return call(
        kernel,
        array(N, 2 * ROWS, 128),
        800_000_000,
        5_500_000,
        vmem=60,
        grid=(steps,),
        in_specs=[
            pl.BlockSpec((2 * R, MINE * QLEN), lambda n: (0, 0)),
            pl.BlockSpec((2 * R, MINE * PLEN), lambda n: (0, 0)),
            pl.BlockSpec((MINE * QLEN, cols), lambda n: (0, n)),
            pl.BlockSpec((MINE * PLEN, cols), lambda n: (0, n)),
        ],
        out_specs=pl.BlockSpec((N // steps, 2 * ROWS, 128), lambda n: (n, 0, 0)),
        scratch_shapes=[pltpu.VMEM((2 * ROWS, MINE * QLEN), BF), pltpu.VMEM((2 * ROWS, MINE * PLEN), BF)],
    )(q_fact.T, p_fact.T, q_cot, p_cot)


def permuted(projection):
    def kernel(proj, out, order):
        @pl.when(pl.program_id(0) == 0)
        def _():
            u, v = iota((G, G), 0), iota((G, G), 1)
            order[...] = ones_where(v == (u & 63) * 16 + ((u >> 6) & 1) * 8 + (u >> 7))

        out[...] = dot(order[...], proj[...]).astype(BF)

    tile = pl.BlockSpec((G, 512), lambda n: (0, n))
    return call(
        kernel,
        array(G, K),
        2 * G * G * K,
        16_000_000,
        vmem=60,
        grid=(K // 512,),
        in_specs=[tile],
        out_specs=tile,
        scratch_shapes=[pltpu.VMEM((G, G), BF)],
    )(projection)


def rows_of(recv, kind, at, count):
    pieces = []
    while count:
        src, off = at // ROWS, at % ROWS
        take = min(ROWS - off, count)
        pieces.append(recv[src, kind * ROWS + off : kind * ROWS + off + take, :])
        at, count = at + take, count - take
    return jnp.concatenate(pieces, axis=0)


def halves(pair, proj, outs):
    part = dot(pair[...], proj[...]).astype(BF)
    for d in range(NX):
        outs[d][...] = part[ROWS * d : ROWS * d + ROWS, :]


def product_left(recv, passage_of, proj):
    def kernel(recv, passage, proj, pair, o0, o1, o2, o3, wide_q, wide_p, held, sem):
        copy = pltpu.make_async_copy(proj.at[:, : K // 2], held, sem)
        copy.start()
        x = lax.axis_index("px")
        r, c = iota((256, 256), 0), iota((256, 256), 1)
        swap = ones_where(c == (r & 31) * 8 + (r >> 5))
        for g in range(PAIRS // 32):
            both = jnp.concatenate([rows_of(recv, kind, 256 * g, 256) for kind in range(2)], axis=1)
            mixed = dot(swap, both).astype(BF)
            for b in range(8):
                wide_q[32 * g : 32 * g + 32, 128 * b : 128 * b + 128] = mixed[32 * b : 32 * b + 32, :128]
                wide_p[32 * g : 32 * g + 32, 128 * b : 128 * b + 128] = mixed[32 * b : 32 * b + 32, 128:]
        hot = ones_where(iota((PAIRS, PAIRS), 0) == passage[...])
        picked = lax.dot_general(hot, wide_p[...], (((0,), (0,)), ((), ())), preferred_element_type=F32)
        summed = (wide_q[...].astype(F32) + picked).astype(BF)
        for i in range(NX):
            at = pl.multiple_of(((i - x) & 3) * ROWS, 32)
            pair[pl.ds(at, ROWS), :] = summed[ROWS * i : ROWS * i + ROWS, :]
        copy.wait()
        halves(pair, held, (o0, o1, o2, o3))

    return call(
        kernel,
        [array(PAIRS, G)] + [array(ROWS, K // 2)] * 4,
        2_500_000_000,
        8_000_000,
        in_specs=[WHOLE, WHOLE, HBM],
        scratch_shapes=[
            pltpu.VMEM((PAIRS, G), BF),
            pltpu.VMEM((PAIRS, G), BF),
            pltpu.VMEM((G, K // 2), BF),
            pltpu.SemaphoreType.DMA,
        ],
    )(recv, passage_of.reshape(1, PAIRS), proj)


def product_right(pair, proj):
    def kernel(pair, proj, o0, o1, o2, o3, held, sems):
        copies = []
        for i in range(2):
            at = pl.ds(K // 2 + KV * i, KV)
            copies.append(pltpu.make_async_copy(proj.at[:, at], held.at[i], sems.at[i]))
            copies[i].start()
        for i in range(2):
            copies[i].wait()
            part = dot(pair[...], held[i]).astype(BF)
            for d, out in enumerate((o0, o1, o2, o3)):
                out[:, KV * i : KV * i + KV] = part[ROWS * d : ROWS * d + ROWS, :]

    return call(
        kernel,
        [array(ROWS, K // 2)] * 4,
        1_700_000_000,
        7_000_000,
        in_specs=[WHOLE, HBM],
        scratch_shapes=[pltpu.VMEM((2, G, KV), BF), pltpu.SemaphoreType.DMA((2,))],
    )(pair, proj)


def add(a, b):
    return (a.astype(F32) + b.astype(F32)).astype(BF)


def shift(x, axis, size, by):
    return lax.ppermute(x, axis, [(i, (i + by) % size) for i in range(size)])


def across_x(left, right):
    l0, l1, l2, l3 = left
    r0, r1, r2, r3 = right
    far_l = shift(l2, "px", NX, 1)
    got_l = shift(l3, "px", NX, -1)
    far_r = shift(r2, "px", NX, -1)
    got_r = shift(r1, "px", NX, 1)
    sum_l = shift(add(l1, far_l), "px", NX, 1)
    sum_r = shift(add(r3, far_r), "px", NX, -1)
    return l0, got_l, sum_l, r0, got_r, sum_r


def across_z(terms):
    def kernel(l0, l1, l2, r0, r1, r2, *outs):
        left = (l0[...].astype(F32) + l1[...].astype(F32) + l2[...].astype(F32)).astype(BF)
        right = (r0[...].astype(F32) + r1[...].astype(F32) + r2[...].astype(F32)).astype(BF)
        stacked = jnp.concatenate([left[:, :KV], left[:, KV:], right[:, :KV], right[:, KV:]], axis=0)
        r, c = iota((4 * ROWS, 4 * ROWS), 0), iota((4 * ROWS, 4 * ROWS), 1)
        block = r // 48
        quarter = (r - block * 48) // MINE
        item = r - block * 48 - quarter * MINE
        z = (block + lax.axis_index("pz")) & (NZ - 1)
        hot = ones_where(c == quarter * ROWS + z * MINE + item)
        rows = dot(hot, stacked).astype(BF)
        for k in range(NZ):
            outs[k][...] = rows[48 * k : 48 * k + 48, :]

    blocks = call(kernel, [array(48, KV)] * NZ, 300_000_000, 4_000_000)(*terms)
    return [blocks[0]] + [shift(blocks[k], "pz", NZ, k) for k in (4, 3, 5, 2, 6, 1, 7)]


def last_sum(parts):
    def kernel(*refs):
        out = refs[NZ]
        total = refs[0][...].astype(F32)
        for i in range(1, NZ):
            total = total + refs[i][...].astype(F32)
        for q in range(4):
            out[:, KV * q : KV * q + KV] = total[MINE * q : MINE * q + MINE, :]

    return call(kernel, array(MINE, K, dtype=F32), 1_000_000, 1_000_000)(*parts)


def local(q_fact, p_fact, q_cot, p_cot, passage_of, projection):
    recv = lax.all_to_all(grads(q_fact, p_fact, q_cot, p_cot), ("px", "pz"), 0, 0, tiled=True)
    proj = permuted(projection)
    pair, *left = product_left(recv, passage_of, proj)
    return last_sum(across_z(across_x(left, product_right(pair, proj))))


def solution(mesh):
    cut = Mesh(mesh.devices.reshape(mesh.shape["pairs"], NX, NZ), ("pairs", "px", "pz"))
    rows = P(("pairs", "px", "pz"), None)
    return jax.shard_map(
        local,
        mesh=cut,
        in_specs=(rows, rows, rows, rows, P("pairs"), P(("px", "pz"), None)),
        out_specs=rows,
        check_vma=False,
    )
```

```python
import jax
import jax.numpy as jnp
from jax import lax
from jax.experimental import pallas as pl
from jax.experimental.pallas import tpu as pltpu
from jax.sharding import Mesh, PartitionSpec as P

KV = 1024
R = 16
QLEN = 32
PLEN = 48
K = 4096
NX, NZ = 4, 8
N = NX * NZ
MINE = 12
PAIRS = N * MINE
G = 1024
ROWS = MINE * 8
MIB = 1024 * 1024
BF = jnp.bfloat16
F32 = jnp.float32
HBM = pl.BlockSpec(memory_space=pltpu.HBM)
WHOLE = pl.BlockSpec(memory_space=pltpu.VMEM)


def iota(shape, dim):
    return lax.broadcasted_iota(jnp.int32, shape, dim)


def dot(a, b):
    return lax.dot_general(a, b, (((1,), (0,)), ((), ())), preferred_element_type=F32)


def ones_where(mask):
    return jnp.where(mask, 1.0, 0.0).astype(BF)


def call(kernel, out_shape, flops, moved, vmem=24, **kwargs):
    return pl.pallas_call(
        kernel,
        out_shape=out_shape,
        compiler_params=pltpu.CompilerParams(vmem_limit_bytes=vmem * MIB),
        cost_estimate=pl.CostEstimate(flops=flops, bytes_accessed=moved, transcendentals=0),
        **kwargs,
    )


def array(*shape, dtype=BF):
    return jax.ShapeDtypeStruct(shape, dtype)


def grads(q_fact, p_fact, q_cot, p_cot):
    steps = 4
    cols = 2 * KV // steps
    dests = N // steps

    def kernel(q_fact, p_fact, q_cot, p_cot, out, q_held, p_held, made, in_sems, out_sems):
        def load(kind, n):
            cot, held = ((q_cot, q_held), (p_cot, p_held))[kind]
            return pltpu.make_async_copy(cot.at[:, pl.ds(cols * n, cols)], held.at[n], in_sems.at[kind, n])

        def store(n):
            at = pl.ds(dests * n, dests)
            return pltpu.make_async_copy(made.at[at], out.at[at], out_sems.at[n])

        for n in range(steps):
            for kind in range(2):
                load(kind, n).start()
        lane = iota((ROWS, 128), 1)
        spreads = []
        for layer in range(2):
            for fact, length in ((q_fact, QLEN), (p_fact, PLEN)):
                tokens = MINE * length
                row = iota((2 * ROWS, R), 0)
                rank = jnp.where(row >= ROWS, 8, 0) + (row & 7)
                pick = ones_where(iota((2 * ROWS, R), 1) == rank)
                row = iota((2 * ROWS, tokens), 0)
                item = jnp.where(row >= ROWS, row - ROWS, row) >> 3
                token = iota((2 * ROWS, tokens), 1) - item * length
                held = (token >= 0) & (token < length)
                rows = dot(pick, fact[R * layer : R * layer + R, :])
                spreads.append(jnp.where(held, rows, 0.0).astype(BF))
        for n in range(steps):
            for kind, held in enumerate((q_held, p_held)):
                load(kind, n).wait()
                grad = dot(spreads[2 * (2 * n // steps) + kind], held[n])
                for j in range(cols // 128):
                    top = grad[:ROWS, 128 * j : 128 * j + 128]
                    low = grad[ROWS:, 128 * j : 128 * j + 128]
                    at = pl.ds(kind * ROWS, ROWS)
                    dest = dests * n + 2 * j
                    made[dest, at, :] = jnp.where(lane < 64, top, pltpu.roll(low, 64, 1)).astype(BF)
                    made[dest + 1, at, :] = jnp.where(lane < 64, pltpu.roll(top, 64, 1), low).astype(BF)
            store(n).start()
        for n in range(steps):
            store(n).wait()

    return call(
        kernel,
        array(N, 2 * ROWS, 128),
        800_000_000,
        5_500_000,
        vmem=60,
        in_specs=[WHOLE, WHOLE, HBM, HBM],
        out_specs=HBM,
        scratch_shapes=[
            pltpu.VMEM((steps, MINE * QLEN, cols), BF),
            pltpu.VMEM((steps, MINE * PLEN, cols), BF),
            pltpu.VMEM((N, 2 * ROWS, 128), BF),
            pltpu.SemaphoreType.DMA((2, steps)),
            pltpu.SemaphoreType.DMA((steps,)),
        ],
    )(q_fact.T, p_fact.T, q_cot, p_cot)


def prepared(projection, passage_of):
    steps = 8
    cols = K // steps

    def kernel(passage, proj, out, hot, held, made, order, in_sems, out_sems):
        def load(n):
            return pltpu.make_async_copy(proj.at[:, pl.ds(cols * n, cols)], held.at[n], in_sems.at[n])

        def store(n):
            return pltpu.make_async_copy(made.at[n], out.at[:, pl.ds(cols * n, cols)], out_sems.at[n])

        for n in range(steps):
            load(n).start()
        hot[...] = ones_where(iota((PAIRS, PAIRS), 1) == passage[...])
        u, v = iota((G, G), 0), iota((G, G), 1)
        order[...] = ones_where(v == (u & 63) * 16 + ((u >> 6) & 1) * 8 + (u >> 7))
        for n in range(steps):
            load(n).wait()
            made[n] = dot(order[...], held[n]).astype(BF)
            store(n).start()
        for n in range(steps):
            store(n).wait()

    return call(
        kernel,
        [array(G, K), array(PAIRS, PAIRS)],
        2 * G * G * K,
        16_000_000,
        vmem=32,
        in_specs=[WHOLE, HBM],
        out_specs=[HBM, WHOLE],
        scratch_shapes=[
            pltpu.VMEM((steps, G, cols), BF),
            pltpu.VMEM((steps, G, cols), BF),
            pltpu.VMEM((G, G), BF),
            pltpu.SemaphoreType.DMA((steps,)),
            pltpu.SemaphoreType.DMA((steps,)),
        ],
    )(passage_of.reshape(PAIRS, 1), projection)


def rows_of(recv, kind, at, count):
    pieces = []
    while count:
        src, off = at // ROWS, at % ROWS
        take = min(ROWS - off, count)
        pieces.append(recv[src, kind * ROWS + off : kind * ROWS + off + take, :])
        at, count = at + take, count - take
    return jnp.concatenate(pieces, axis=0)


def parts(pair, proj, held, sems, takes):
    for i in range(4):
        pltpu.make_async_copy(proj.at[:, pl.ds(KV * i, KV)], held.at[i], sems.at[i]).wait()
        first, outs = takes[i // 2]
        part = dot(pair[ROWS * first : ROWS * (first + len(outs)), :], held[i]).astype(BF)
        for j, out in enumerate(outs):
            out[:, KV * (i % 2) : KV * (i % 2) + KV] = part[ROWS * j : ROWS * j + ROWS, :]


def fetch(proj, held, sems):
    for i in range(4):
        pltpu.make_async_copy(proj.at[:, pl.ds(KV * i, KV)], held.at[i], sems.at[i]).start()


QUARTERS = [pltpu.VMEM((4, G, KV), BF), pltpu.SemaphoreType.DMA((4,))]


def product_far(recv, hot, proj):
    def kernel(recv, hot, proj, pair, l1, l2, r2, r3, wide_q, wide_p, held, sems):
        fetch(proj, held, sems)
        x = lax.axis_index("px")
        r, c = iota((256, 256), 0), iota((256, 256), 1)
        swap = ones_where(c == (r & 31) * 8 + (r >> 5))
        for g in range(PAIRS // 32):
            both = jnp.concatenate([rows_of(recv, kind, 256 * g, 256) for kind in range(2)], axis=1)
            mixed = dot(swap, both).astype(BF)
            for b in range(8):
                wide_q[32 * g : 32 * g + 32, 128 * b : 128 * b + 128] = mixed[32 * b : 32 * b + 32, :128]
                wide_p[32 * g : 32 * g + 32, 128 * b : 128 * b + 128] = mixed[32 * b : 32 * b + 32, 128:]
        summed = (wide_q[...].astype(F32) + dot(hot[...], wide_p[...])).astype(BF)
        for i in range(NX):
            at = pl.multiple_of(((i - x) & 3) * ROWS, 32)
            pair[pl.ds(at, ROWS), :] = summed[ROWS * i : ROWS * i + ROWS, :]
        parts(pair, proj, held, sems, ((1, (l1, l2)), (2, (r2, r3))))

    return call(
        kernel,
        [array(PAIRS, G)] + [array(ROWS, K // 2)] * 4,
        2_500_000_000,
        12_000_000,
        in_specs=[WHOLE, WHOLE, HBM],
        scratch_shapes=[pltpu.VMEM((PAIRS, G), BF), pltpu.VMEM((PAIRS, G), BF)] + QUARTERS,
    )(recv, hot, proj)


def product_near(pair, proj):
    def kernel(pair, proj, l0, l3, r0, r1, turned, held, sems):
        fetch(proj, held, sems)
        turned[:ROWS, :] = pair[3 * ROWS :, :]
        turned[ROWS:, :] = pair[: 3 * ROWS, :]
        parts(turned, proj, held, sems, ((0, (l3, l0)), (1, (r0, r1))))

    return call(
        kernel,
        [array(ROWS, K // 2)] * 4,
        1_700_000_000,
        10_000_000,
        in_specs=[WHOLE, HBM],
        scratch_shapes=[pltpu.VMEM((PAIRS, G), BF)] + QUARTERS,
    )(pair, proj)


def add(a, b):
    return (a.astype(F32) + b.astype(F32)).astype(BF)


def shift(x, axis, size, by):
    return lax.ppermute(x, axis, [(i, (i + by) % size) for i in range(size)])


def across_x(recv, hot, proj):
    pair, l1, l2, r2, r3 = product_far(recv, hot, proj)
    far_l = shift(l2, "px", NX, 1)
    far_r = shift(r2, "px", NX, -1)
    l0, l3, r0, r1 = product_near(pair, proj)
    got_l = shift(l3, "px", NX, -1)
    got_r = shift(r1, "px", NX, 1)
    sum_l = shift(add(l1, far_l), "px", NX, 1)
    sum_r = shift(add(r3, far_r), "px", NX, -1)
    return l0, got_l, sum_l, r0, got_r, sum_r


def across_z(terms):
    def kernel(l0, l1, l2, r0, r1, r2, *outs):
        left = (l0[...].astype(F32) + l1[...].astype(F32) + l2[...].astype(F32)).astype(BF)
        right = (r0[...].astype(F32) + r1[...].astype(F32) + r2[...].astype(F32)).astype(BF)
        stacked = jnp.concatenate([left[:, :KV], left[:, KV:], right[:, :KV], right[:, KV:]], axis=0)
        r, c = iota((4 * ROWS, 4 * ROWS), 0), iota((4 * ROWS, 4 * ROWS), 1)
        block = r // 48
        quarter = (r - block * 48) // MINE
        item = r - block * 48 - quarter * MINE
        z = (block + lax.axis_index("pz")) & (NZ - 1)
        hot = ones_where(c == quarter * ROWS + z * MINE + item)
        rows = dot(hot, stacked).astype(BF)
        for k in range(NZ):
            outs[k][...] = rows[48 * k : 48 * k + 48, :]

    blocks = call(kernel, [array(48, KV)] * NZ, 300_000_000, 4_000_000)(*terms)
    return [blocks[0]] + [shift(blocks[k], "pz", NZ, k) for k in (4, 3, 5, 2, 6, 1, 7)]


def last_sum(parts):
    def kernel(*refs):
        out = refs[NZ]
        total = refs[0][...].astype(F32)
        for i in range(1, NZ):
            total = total + refs[i][...].astype(F32)
        for q in range(4):
            out[:, KV * q : KV * q + KV] = total[MINE * q : MINE * q + MINE, :]

    return call(kernel, array(MINE, K, dtype=F32), 1_000_000, 1_000_000)(*parts)


def local(q_fact, p_fact, q_cot, p_cot, passage_of, projection):
    recv = lax.all_to_all(grads(q_fact, p_fact, q_cot, p_cot), ("px", "pz"), 0, 0, tiled=True)
    proj, hot = prepared(projection, passage_of)
    return last_sum(across_z(across_x(recv, hot, proj)))


def solution(mesh):
    cut = Mesh(mesh.devices.reshape(mesh.shape["pairs"], NX, NZ), ("pairs", "px", "pz"))
    rows = P(("pairs", "px", "pz"), None)
    return jax.shard_map(
        local,
        mesh=cut,
        in_specs=(rows, rows, rows, rows, P("pairs"), P(("px", "pz"), None)),
        out_specs=rows,
        check_vma=False,
    )
```

```python
import jax
import jax.numpy as jnp
from jax import lax
from jax.experimental import pallas as pl
from jax.experimental.pallas import tpu as pltpu
from jax.sharding import Mesh, PartitionSpec as P

KV = 1024
R = 16
QLEN = 32
PLEN = 48
K = 4096
NX, NZ = 4, 8
N = NX * NZ
MINE = 12
PAIRS = N * MINE
G = 1024
ROWS = MINE * 8
MIB = 1024 * 1024
BF = jnp.bfloat16
F32 = jnp.float32
HBM = pl.BlockSpec(memory_space=pltpu.HBM)
WHOLE = pl.BlockSpec(memory_space=pltpu.VMEM)


def iota(shape, dim):
    return lax.broadcasted_iota(jnp.int32, shape, dim)


def dot(a, b):
    return lax.dot_general(a, b, (((1,), (0,)), ((), ())), preferred_element_type=F32)


def ones_where(mask):
    return jnp.where(mask, 1.0, 0.0).astype(BF)


def call(kernel, out_shape, flops, moved, vmem=24, **kwargs):
    return pl.pallas_call(
        kernel,
        out_shape=out_shape,
        compiler_params=pltpu.CompilerParams(vmem_limit_bytes=vmem * MIB),
        cost_estimate=pl.CostEstimate(flops=flops, bytes_accessed=moved, transcendentals=0),
        **kwargs,
    )


def array(*shape, dtype=BF):
    return jax.ShapeDtypeStruct(shape, dtype)


def grads(q_fact, p_fact, q_cot, p_cot):
    steps = 2
    cols = 2 * KV // steps

    def kernel(q_fact, p_fact, q_cot, p_cot, out, q_spread, p_spread):
        step = pl.program_id(0)
        lane = iota((ROWS, 128), 1)
        for kind, (fact, cot, length, spread) in enumerate(
            ((q_fact, q_cot, QLEN, q_spread), (p_fact, p_cot, PLEN, p_spread))
        ):
            tokens = MINE * length

            @pl.when(step % (steps // 2) == 0)
            def _():
                row = iota((2 * ROWS, 2 * R), 0)
                rank = jnp.where(row >= ROWS, 8, 0) + (row & 7) + (step // (steps // 2)) * R
                pick = ones_where(iota((2 * ROWS, 2 * R), 1) == rank)
                row = iota((2 * ROWS, tokens), 0)
                item = jnp.where(row >= ROWS, row - ROWS, row) >> 3
                token = iota((2 * ROWS, tokens), 1) - item * length
                held = (token >= 0) & (token < length)
                spread[...] = jnp.where(held, dot(pick, fact[...]), 0.0).astype(BF)

            grad = dot(spread[...], cot[...])
            for j in range(cols // 128):
                top = grad[:ROWS, 128 * j : 128 * j + 128]
                low = grad[ROWS:, 128 * j : 128 * j + 128]
                at = pl.ds(kind * ROWS, ROWS)
                out[2 * j, at, :] = jnp.where(lane < 64, top, pltpu.roll(low, 64, 1)).astype(BF)
                out[2 * j + 1, at, :] = jnp.where(lane < 64, pltpu.roll(top, 64, 1), low).astype(BF)

    return call(
        kernel,
        array(N, 2 * ROWS, 128),
        800_000_000,
        5_500_000,
        vmem=60,
        grid=(steps,),
        in_specs=[
            pl.BlockSpec((2 * R, MINE * QLEN), lambda n: (0, 0)),
            pl.BlockSpec((2 * R, MINE * PLEN), lambda n: (0, 0)),
            pl.BlockSpec((MINE * QLEN, cols), lambda n: (0, n)),
            pl.BlockSpec((MINE * PLEN, cols), lambda n: (0, n)),
        ],
        out_specs=pl.BlockSpec((N // steps, 2 * ROWS, 128), lambda n: (n, 0, 0)),
        scratch_shapes=[pltpu.VMEM((2 * ROWS, MINE * QLEN), BF), pltpu.VMEM((2 * ROWS, MINE * PLEN), BF)],
    )(q_fact.T, p_fact.T, q_cot, p_cot)


def prepared(projection, passage_of):
    steps = 8
    cols = K // steps

    def kernel(passage, proj, out, hot, held, made, order, in_sems, out_sems):
        def load(n):
            return pltpu.make_async_copy(proj.at[:, pl.ds(cols * n, cols)], held.at[n], in_sems.at[n])

        def store(n):
            return pltpu.make_async_copy(made.at[n], out.at[:, pl.ds(cols * n, cols)], out_sems.at[n])

        for n in range(steps):
            load(n).start()
        hot[...] = ones_where(iota((PAIRS, PAIRS), 1) == passage[...])
        u, v = iota((G, G), 0), iota((G, G), 1)
        order[...] = ones_where(v == (u & 63) * 16 + ((u >> 6) & 1) * 8 + (u >> 7))
        for n in range(steps):
            load(n).wait()
            made[n] = dot(order[...], held[n]).astype(BF)
            store(n).start()
        for n in range(steps):
            store(n).wait()

    return call(
        kernel,
        [array(G, K), array(PAIRS, PAIRS)],
        2 * G * G * K,
        16_000_000,
        vmem=57,
        in_specs=[WHOLE, HBM],
        out_specs=[HBM, WHOLE],
        scratch_shapes=[
            pltpu.VMEM((steps, G, cols), BF),
            pltpu.VMEM((steps, G, cols), BF),
            pltpu.VMEM((G, G), BF),
            pltpu.SemaphoreType.DMA((steps,)),
            pltpu.SemaphoreType.DMA((steps,)),
        ],
    )(passage_of.reshape(PAIRS, 1), projection)


def rows_of(recv, kind, at, count):
    pieces = []
    while count:
        src, off = at // ROWS, at % ROWS
        take = min(ROWS - off, count)
        pieces.append(recv[src, kind * ROWS + off : kind * ROWS + off + take, :])
        at, count = at + take, count - take
    return jnp.concatenate(pieces, axis=0)


def product(recv, hot, proj):
    def kernel(recv, hot, proj, l0, l1, l2, l3, r0, r1, r2, r3, wide_q, wide_p, pair, held, sems):
        def load(n):
            return pltpu.make_async_copy(proj.at[:, pl.ds(KV * n, KV)], held.at[n], sems.at[n])

        for n in range(4):
            load(n).start()
        x = lax.axis_index("px")
        r, c = iota((256, 256), 0), iota((256, 256), 1)
        swap = ones_where(c == (r & 31) * 8 + (r >> 5))
        for g in range(PAIRS // 32):
            both = jnp.concatenate([rows_of(recv, kind, 256 * g, 256) for kind in range(2)], axis=1)
            mixed = dot(swap, both).astype(BF)
            for b in range(8):
                wide_q[32 * g : 32 * g + 32, 128 * b : 128 * b + 128] = mixed[32 * b : 32 * b + 32, :128]
                wide_p[32 * g : 32 * g + 32, 128 * b : 128 * b + 128] = mixed[32 * b : 32 * b + 32, 128:]
        summed = (wide_q[...].astype(F32) + dot(hot[...], wide_p[...])).astype(BF)
        for i in range(NX):
            at = pl.multiple_of(((i - x) & 3) * ROWS, 32)
            pair[pl.ds(at, ROWS), :] = summed[ROWS * i : ROWS * i + ROWS, :]
        for n in range(4):
            load(n).wait()
            part = dot(pair[...], held[n]).astype(BF)
            at = KV * (n % 2)
            for d, out in enumerate(((l0, l1, l2, l3), (r0, r1, r2, r3))[n // 2]):
                out[:, at : at + KV] = part[ROWS * d : ROWS * d + ROWS, :]

    return call(
        kernel,
        [array(ROWS, K // 2)] * 8,
        4_000_000_000,
        14_000_000,
        vmem=57,
        in_specs=[WHOLE, WHOLE, HBM],
        scratch_shapes=[pltpu.VMEM((PAIRS, G), BF)] * 3
        + [pltpu.VMEM((4, G, KV), BF), pltpu.SemaphoreType.DMA((4,))],
    )(recv, hot, proj)


def add(a, b):
    return (a.astype(F32) + b.astype(F32)).astype(BF)


def shift(x, axis, size, by):
    return lax.ppermute(x, axis, [(i, (i + by) % size) for i in range(size)])


def across_x(blocks):
    l0, l1, l2, l3, r0, r1, r2, r3 = blocks
    far_l = shift(l2, "px", NX, 1)
    far_r = shift(r2, "px", NX, -1)
    got_l = shift(l3, "px", NX, -1)
    got_r = shift(r1, "px", NX, 1)
    sum_l = shift(add(l1, far_l), "px", NX, 1)
    sum_r = shift(add(r3, far_r), "px", NX, -1)
    return l0, got_l, sum_l, r0, got_r, sum_r


def across_z(terms):
    def kernel(l0, l1, l2, r0, r1, r2, *outs):
        left = (l0[...].astype(F32) + l1[...].astype(F32) + l2[...].astype(F32)).astype(BF)
        right = (r0[...].astype(F32) + r1[...].astype(F32) + r2[...].astype(F32)).astype(BF)
        stacked = jnp.concatenate([left[:, :KV], left[:, KV:], right[:, :KV], right[:, KV:]], axis=0)
        r, c = iota((4 * ROWS, 4 * ROWS), 0), iota((4 * ROWS, 4 * ROWS), 1)
        block = r // 48
        quarter = (r - block * 48) // MINE
        item = r - block * 48 - quarter * MINE
        z = (block + lax.axis_index("pz")) & (NZ - 1)
        hot = ones_where(c == quarter * ROWS + z * MINE + item)
        rows = dot(hot, stacked).astype(BF)
        for k in range(NZ):
            outs[k][...] = rows[48 * k : 48 * k + 48, :]

    blocks = call(kernel, [array(48, KV)] * NZ, 300_000_000, 4_000_000)(*terms)
    return [blocks[0]] + [shift(blocks[k], "pz", NZ, k) for k in (4, 3, 5, 2, 6, 1, 7)]


def last_sum(parts):
    def kernel(*refs):
        out = refs[NZ]
        total = refs[0][...].astype(F32)
        for i in range(1, NZ):
            total = total + refs[i][...].astype(F32)
        for q in range(4):
            out[:, KV * q : KV * q + KV] = total[MINE * q : MINE * q + MINE, :]

    return call(kernel, array(MINE, K, dtype=F32), 1_000_000, 1_000_000)(*parts)


def local(q_fact, p_fact, q_cot, p_cot, passage_of, projection):
    recv = lax.all_to_all(grads(q_fact, p_fact, q_cot, p_cot), ("px", "pz"), 0, 0, tiled=True)
    proj, hot = prepared(projection, passage_of)
    return last_sum(across_z(across_x(product(recv, hot, proj))))


def solution(mesh):
    cut = Mesh(mesh.devices.reshape(mesh.shape["pairs"], NX, NZ), ("pairs", "px", "pz"))
    rows = P(("pairs", "px", "pz"), None)
    return jax.shard_map(
        local,
        mesh=cut,
        in_specs=(rows, rows, rows, rows, P("pairs"), P(("px", "pz"), None)),
        out_specs=rows,
        check_vma=False,
    )
```

```python
import jax
import jax.numpy as jnp
from jax import lax
from jax.experimental import pallas as pl
from jax.experimental.pallas import tpu as pltpu
from jax.sharding import Mesh, PartitionSpec as P

KV = 1024
R = 16
QLEN = 32
PLEN = 48
K = 4096
NX, NZ = 4, 8
N = NX * NZ
MINE = 12
PAIRS = N * MINE
G = 1024
ROWS = MINE * 8
MIB = 1024 * 1024
BF = jnp.bfloat16
F32 = jnp.float32
HBM = pl.BlockSpec(memory_space=pltpu.HBM)
WHOLE = pl.BlockSpec(memory_space=pltpu.VMEM)


def iota(shape, dim):
    return lax.broadcasted_iota(jnp.int32, shape, dim)


def dot(a, b):
    return lax.dot_general(a, b, (((1,), (0,)), ((), ())), preferred_element_type=F32)


def ones_where(mask):
    return jnp.where(mask, 1.0, 0.0).astype(BF)


def call(kernel, out_shape, flops, moved, vmem=24, **kwargs):
    return pl.pallas_call(
        kernel,
        out_shape=out_shape,
        compiler_params=pltpu.CompilerParams(vmem_limit_bytes=vmem * MIB),
        cost_estimate=pl.CostEstimate(flops=flops, bytes_accessed=moved, transcendentals=0),
        **kwargs,
    )


def array(*shape, dtype=BF):
    return jax.ShapeDtypeStruct(shape, dtype)


def grads(q_fact, p_fact, q_cot, p_cot):
    steps = 2
    cols = 2 * KV // steps

    def kernel(q_fact, p_fact, q_cot, p_cot, out, q_spread, p_spread):
        step = pl.program_id(0)
        lane = iota((ROWS, 128), 1)
        for kind, (fact, cot, length, spread) in enumerate(
            ((q_fact, q_cot, QLEN, q_spread), (p_fact, p_cot, PLEN, p_spread))
        ):
            tokens = MINE * length

            @pl.when(step % (steps // 2) == 0)
            def _():
                row = iota((2 * ROWS, 2 * R), 0)
                rank = jnp.where(row >= ROWS, 8, 0) + (row & 7) + (step // (steps // 2)) * R
                pick = ones_where(iota((2 * ROWS, 2 * R), 1) == rank)
                row = iota((2 * ROWS, tokens), 0)
                item = jnp.where(row >= ROWS, row - ROWS, row) >> 3
                token = iota((2 * ROWS, tokens), 1) - item * length
                held = (token >= 0) & (token < length)
                spread[...] = jnp.where(held, dot(pick, fact[...]), 0.0).astype(BF)

            grad = dot(spread[...], cot[...])
            for j in range(cols // 128):
                top = grad[:ROWS, 128 * j : 128 * j + 128]
                low = grad[ROWS:, 128 * j : 128 * j + 128]
                at = pl.ds(kind * ROWS, ROWS)
                out[2 * j, at, :] = jnp.where(lane < 64, top, pltpu.roll(low, 64, 1)).astype(BF)
                out[2 * j + 1, at, :] = jnp.where(lane < 64, pltpu.roll(top, 64, 1), low).astype(BF)

    return call(
        kernel,
        array(N, 2 * ROWS, 128),
        800_000_000,
        5_500_000,
        vmem=60,
        grid=(steps,),
        in_specs=[
            pl.BlockSpec((2 * R, MINE * QLEN), lambda n: (0, 0)),
            pl.BlockSpec((2 * R, MINE * PLEN), lambda n: (0, 0)),
            pl.BlockSpec((MINE * QLEN, cols), lambda n: (0, n)),
            pl.BlockSpec((MINE * PLEN, cols), lambda n: (0, n)),
        ],
        out_specs=pl.BlockSpec((N // steps, 2 * ROWS, 128), lambda n: (n, 0, 0)),
        scratch_shapes=[pltpu.VMEM((2 * ROWS, MINE * QLEN), BF), pltpu.VMEM((2 * ROWS, MINE * PLEN), BF)],
    )(q_fact.T, p_fact.T, q_cot, p_cot)


def prepared(projection, passage_of):
    steps = 8
    cols = K // steps

    def kernel(passage, proj, out, hot, held, made, order, in_sems, out_sems):
        def load(n):
            return pltpu.make_async_copy(proj.at[:, pl.ds(cols * n, cols)], held.at[n], in_sems.at[n])

        def store(n):
            return pltpu.make_async_copy(made.at[n], out.at[:G, pl.ds(cols * n, cols)], out_sems.at[n])

        for n in range(steps):
            load(n).start()
        hot[...] = ones_where(iota((PAIRS, PAIRS), 1) == passage[...])
        u, v = iota((G, G), 0), iota((G, G), 1)
        order[...] = ones_where(v == (u & 63) * 16 + ((u >> 6) & 1) * 8 + (u >> 7))
        for n in range(steps):
            load(n).wait()
            made[n] = dot(order[...], held[n]).astype(BF)
            store(n).start()
        for n in range(steps):
            store(n).wait()

    return call(
        kernel,
        [array(3 * G, K), array(PAIRS, PAIRS)],
        2 * G * G * K,
        16_000_000,
        vmem=57,
        in_specs=[WHOLE, HBM],
        out_specs=[HBM, WHOLE],
        scratch_shapes=[
            pltpu.VMEM((steps, G, cols), BF),
            pltpu.VMEM((steps, G, cols), BF),
            pltpu.VMEM((G, G), BF),
            pltpu.SemaphoreType.DMA((steps,)),
            pltpu.SemaphoreType.DMA((steps,)),
        ],
    )(passage_of.reshape(PAIRS, 1), projection)


def rows_of(recv, kind, at, count):
    pieces = []
    while count:
        src, off = at // ROWS, at % ROWS
        take = min(ROWS - off, count)
        pieces.append(recv[src, kind * ROWS + off : kind * ROWS + off + take, :])
        at, count = at + take, count - take
    return jnp.concatenate(pieces, axis=0)


def fetch(proj, held, sems, first):
    copies = []
    for n in range(2):
        at = pl.ds(KV * (first + n), KV)
        copies.append(pltpu.make_async_copy(proj.at[:G, at], held.at[n], sems.at[n]))
        copies[n].start()
    return copies


def products(pair, copies, held, outs):
    for n in range(2):
        copies[n].wait()
        part = dot(pair[...], held[n]).astype(BF)
        for d, out in enumerate(outs):
            out[:, KV * n : KV * n + KV] = part[ROWS * d : ROWS * d + ROWS, :]


HELD = [pltpu.VMEM((2, G, KV), BF), pltpu.SemaphoreType.DMA((2,))]


def product_left(recv, hot, proj):
    def kernel(recv, hot, proj, pair, o0, o1, o2, o3, wide_q, wide_p, held, sems):
        copies = fetch(proj, held, sems, 0)
        x = lax.axis_index("px")
        r, c = iota((256, 256), 0), iota((256, 256), 1)
        swap = ones_where(c == (r & 31) * 8 + (r >> 5))
        for g in range(PAIRS // 32):
            both = jnp.concatenate([rows_of(recv, kind, 256 * g, 256) for kind in range(2)], axis=1)
            mixed = dot(swap, both).astype(BF)
            for b in range(8):
                wide_q[32 * g : 32 * g + 32, 128 * b : 128 * b + 128] = mixed[32 * b : 32 * b + 32, :128]
                wide_p[32 * g : 32 * g + 32, 128 * b : 128 * b + 128] = mixed[32 * b : 32 * b + 32, 128:]
        summed = (wide_q[...].astype(F32) + dot(hot[...], wide_p[...])).astype(BF)
        for i in range(NX):
            at = pl.multiple_of(((i - x) & 3) * ROWS, 32)
            pair[pl.ds(at, ROWS), :] = summed[ROWS * i : ROWS * i + ROWS, :]
        products(pair, copies, held, (o0, o1, o2, o3))

    return call(
        kernel,
        [array(PAIRS, G)] + [array(ROWS, K // 2)] * 4,
        2_500_000_000,
        8_000_000,
        vmem=44,
        in_specs=[WHOLE, WHOLE, HBM],
        scratch_shapes=[pltpu.VMEM((PAIRS, G), BF)] * 2 + HELD,
    )(recv, hot, proj)


def product_right(pair, proj):
    def kernel(pair, proj, o0, o1, o2, o3, held, sems):
        products(pair, fetch(proj, held, sems, 2), held, (o0, o1, o2, o3))

    return call(
        kernel,
        [array(ROWS, K // 2)] * 4,
        1_700_000_000,
        7_000_000,
        vmem=44,
        in_specs=[WHOLE, HBM],
        scratch_shapes=HELD,
    )(pair, proj)


def add(a, b):
    return (a.astype(F32) + b.astype(F32)).astype(BF)


def shift(x, axis, size, by):
    return lax.ppermute(x, axis, [(i, (i + by) % size) for i in range(size)])


def across_x(left, right):
    l0, l1, l2, l3 = left
    r0, r1, r2, r3 = right
    far_l = shift(l2, "px", NX, 1)
    got_l = shift(l3, "px", NX, -1)
    far_r = shift(r2, "px", NX, -1)
    got_r = shift(r1, "px", NX, 1)
    sum_l = shift(add(l1, far_l), "px", NX, 1)
    sum_r = shift(add(r3, far_r), "px", NX, -1)
    return l0, got_l, sum_l, r0, got_r, sum_r


def across_z(terms):
    def kernel(l0, l1, l2, r0, r1, r2, far_up, far_down, own, up1, up2, down1, down2):
        left = (l0[...].astype(F32) + l1[...].astype(F32) + l2[...].astype(F32)).astype(BF)
        right = (r0[...].astype(F32) + r1[...].astype(F32) + r2[...].astype(F32)).astype(BF)
        stacked = jnp.concatenate([left[:, :KV], left[:, KV:], right[:, :KV], right[:, KV:]], axis=0)
        r, c = iota((4 * ROWS, 4 * ROWS), 0), iota((4 * ROWS, 4 * ROWS), 1)
        block = r // 48
        quarter = (r - block * 48) // MINE
        item = r - block * 48 - quarter * MINE
        z = (block + lax.axis_index("pz")) & (NZ - 1)
        hot = ones_where(c == quarter * ROWS + z * MINE + item)
        rows = dot(hot, stacked).astype(BF)
        for k, out in ((0, own), (1, up1), (2, up2), (6, down2), (7, down1)):
            out[...] = rows[48 * k : 48 * k + 48, :]
        half = KV // 2
        far_up[0] = rows[48 * 3 : 48 * 4, :half]
        far_up[1] = rows[48 * 3 : 48 * 4, half:]
        far_up[2] = rows[48 * 4 : 48 * 5, :half]
        far_down[0] = rows[48 * 5 : 48 * 6, :half]
        far_down[1] = rows[48 * 5 : 48 * 6, half:]
        far_down[2] = rows[48 * 4 : 48 * 5, half:]

    outs = [array(3, 48, KV // 2)] * 2 + [array(48, KV)] * 5
    far_up, far_down, *near = call(kernel, outs, 300_000_000, 4_000_000)(*terms)
    far_up = shift(far_up, "pz", NZ, 2)
    far_down = shift(far_down, "pz", NZ, -2)

    def add_kernel(far_up, far_down, up1, up2, down1, down2, *outs):
        half = KV // 2
        for far, near1, near2, out1, out2, side in (
            (far_up, up1, up2, outs[0], outs[1], 0),
            (far_down, down1, down2, outs[2], outs[3], 1),
        ):
            out1[:, :half] = add(near1[:, :half], far[0])
            out1[:, half:] = add(near1[:, half:], far[1])
            for i in range(2):
                at = slice(half * i, half * i + half)
                out2[:, at] = add(near2[:, at], far[2]) if i == side else near2[:, at]

    own, *near = near
    up1, up2, down1, down2 = call(add_kernel, [array(48, KV)] * 4, 1_000_000, 1_000_000)(far_up, far_down, *near)
    up2 = shift(up2, "pz", NZ, 2)
    down2 = shift(down2, "pz", NZ, -2)
    up1 = shift(up1, "pz", NZ, 1)
    down1 = shift(down1, "pz", NZ, -1)
    return own, up1, up2, down1, down2


def last_sum(parts):
    def kernel(*refs):
        *terms, out = refs
        total = terms[0][...].astype(F32)
        for term in terms[1:]:
            total = total + term[...].astype(F32)
        for q in range(4):
            out[:, KV * q : KV * q + KV] = total[MINE * q : MINE * q + MINE, :]

    return call(kernel, array(MINE, K, dtype=F32), 1_000_000, 1_000_000)(*parts)


def local(q_fact, p_fact, q_cot, p_cot, passage_of, projection):
    recv = lax.all_to_all(grads(q_fact, p_fact, q_cot, p_cot), ("px", "pz"), 0, 0, tiled=True)
    proj, hot = prepared(projection, passage_of)
    pair, *left = product_left(recv, hot, proj)
    return last_sum(across_z(across_x(left, product_right(pair, proj))))


def solution(mesh):
    cut = Mesh(mesh.devices.reshape(mesh.shape["pairs"], NX, NZ), ("pairs", "px", "pz"))
    rows = P(("pairs", "px", "pz"), None)
    return jax.shard_map(
        local,
        mesh=cut,
        in_specs=(rows, rows, rows, rows, P("pairs"), P(("px", "pz"), None)),
        out_specs=rows,
        check_vma=False,
    )
```

```python
import jax
import jax.numpy as jnp
from jax import lax
from jax.experimental import pallas as pl
from jax.experimental.pallas import tpu as pltpu
from jax.sharding import Mesh, PartitionSpec as P

KV = 1024
R = 16
QLEN = 32
PLEN = 48
K = 4096
NX, NZ = 4, 8
N = NX * NZ
MINE = 12
PAIRS = N * MINE
G = 1024
ROWS = MINE * 8
MIB = 1024 * 1024
BF = jnp.bfloat16
F32 = jnp.float32
HBM = pl.BlockSpec(memory_space=pltpu.HBM)
WHOLE = pl.BlockSpec(memory_space=pltpu.VMEM)


def iota(shape, dim):
    return lax.broadcasted_iota(jnp.int32, shape, dim)


def dot(a, b):
    return lax.dot_general(a, b, (((1,), (0,)), ((), ())), preferred_element_type=F32)


def ones_where(mask):
    return jnp.where(mask, 1.0, 0.0).astype(BF)


def call(kernel, out_shape, flops, moved, vmem=24, **kwargs):
    return pl.pallas_call(
        kernel,
        out_shape=out_shape,
        compiler_params=pltpu.CompilerParams(vmem_limit_bytes=vmem * MIB),
        cost_estimate=pl.CostEstimate(flops=flops, bytes_accessed=moved, transcendentals=0),
        **kwargs,
    )


def array(*shape, dtype=BF):
    return jax.ShapeDtypeStruct(shape, dtype)


def grads(q_fact, p_fact, q_cot, p_cot):
    steps = 2
    cols = 2 * KV // steps

    def kernel(q_fact, p_fact, q_cot, p_cot, out, q_spread, p_spread):
        step = pl.program_id(0)
        lane = iota((ROWS, 128), 1)
        for kind, (fact, cot, length, spread) in enumerate(
            ((q_fact, q_cot, QLEN, q_spread), (p_fact, p_cot, PLEN, p_spread))
        ):
            tokens = MINE * length

            @pl.when(step % (steps // 2) == 0)
            def _():
                row = iota((2 * ROWS, 2 * R), 0)
                rank = jnp.where(row >= ROWS, 8, 0) + (row & 7) + (step // (steps // 2)) * R
                pick = ones_where(iota((2 * ROWS, 2 * R), 1) == rank)
                row = iota((2 * ROWS, tokens), 0)
                item = jnp.where(row >= ROWS, row - ROWS, row) >> 3
                token = iota((2 * ROWS, tokens), 1) - item * length
                held = (token >= 0) & (token < length)
                spread[...] = jnp.where(held, dot(pick, fact[...]), 0.0).astype(BF)

            grad = dot(spread[...], cot[...])
            for j in range(cols // 128):
                top = grad[:ROWS, 128 * j : 128 * j + 128]
                low = grad[ROWS:, 128 * j : 128 * j + 128]
                at = pl.ds(kind * ROWS, ROWS)
                out[2 * j, at, :] = jnp.where(lane < 64, top, pltpu.roll(low, 64, 1)).astype(BF)
                out[2 * j + 1, at, :] = jnp.where(lane < 64, pltpu.roll(top, 64, 1), low).astype(BF)

    return call(
        kernel,
        array(N, 2 * ROWS, 128),
        800_000_000,
        5_500_000,
        vmem=60,
        grid=(steps,),
        in_specs=[
            pl.BlockSpec((2 * R, MINE * QLEN), lambda n: (0, 0)),
            pl.BlockSpec((2 * R, MINE * PLEN), lambda n: (0, 0)),
            pl.BlockSpec((MINE * QLEN, cols), lambda n: (0, n)),
            pl.BlockSpec((MINE * PLEN, cols), lambda n: (0, n)),
        ],
        out_specs=pl.BlockSpec((N // steps, 2 * ROWS, 128), lambda n: (n, 0, 0)),
        scratch_shapes=[pltpu.VMEM((2 * ROWS, MINE * QLEN), BF), pltpu.VMEM((2 * ROWS, MINE * PLEN), BF)],
    )(q_fact.T, p_fact.T, q_cot, p_cot)


def permuted(projection):
    steps = 8
    cols = K // steps

    def kernel(proj, out, held, made, order, in_sems, out_sems):
        def load(n):
            return pltpu.make_async_copy(proj.at[:, pl.ds(cols * n, cols)], held.at[n], in_sems.at[n])

        def store(n):
            return pltpu.make_async_copy(made.at[n], out.at[:G, pl.ds(cols * n, cols)], out_sems.at[n])

        for n in range(steps):
            load(n).start()
        u, v = iota((G, G), 0), iota((G, G), 1)
        order[...] = ones_where(v == (u & 63) * 16 + ((u >> 6) & 1) * 8 + (u >> 7))
        for n in range(steps):
            load(n).wait()
            made[n] = dot(order[...], held[n]).astype(BF)
            store(n).start()
        for n in range(steps):
            store(n).wait()

    return call(
        kernel,
        array(3 * G, K),
        2 * G * G * K,
        16_000_000,
        vmem=57,
        in_specs=[HBM],
        out_specs=HBM,
        scratch_shapes=[
            pltpu.VMEM((steps, G, cols), BF),
            pltpu.VMEM((steps, G, cols), BF),
            pltpu.VMEM((G, G), BF),
            pltpu.SemaphoreType.DMA((steps,)),
            pltpu.SemaphoreType.DMA((steps,)),
        ],
    )(projection)


def rows_of(recv, kind, at, count):
    pieces = []
    while count:
        src, off = at // ROWS, at % ROWS
        take = min(ROWS - off, count)
        pieces.append(recv[src, kind * ROWS + off : kind * ROWS + off + take, :])
        at, count = at + take, count - take
    return jnp.concatenate(pieces, axis=0)


def fetch(proj, held, sems):
    copies = []
    for n in range(4):
        copies.append(pltpu.make_async_copy(proj.at[:G, pl.ds(KV * n, KV)], held.at[n], sems.at[n]))
        copies[n].start()
    return copies


def products(pair, copies, held, takes):
    for n in range(4):
        copies[n].wait()
        first, outs = takes[n // 2]
        part = dot(pair[ROWS * first : ROWS * (first + len(outs)), :], held[n]).astype(BF)
        at = KV * (n % 2)
        for d, out in enumerate(outs):
            out[:, at : at + KV] = part[ROWS * d : ROWS * d + ROWS, :]


HELD = [pltpu.VMEM((4, G, KV), BF), pltpu.SemaphoreType.DMA((4,))]


def product_far(recv, passage_of, proj):
    def kernel(recv, passage, proj, pair, l1, l2, r2, r3, wide_q, wide_p, held, sems):
        copies = fetch(proj, held, sems)
        x = lax.axis_index("px")
        r, c = iota((256, 256), 0), iota((256, 256), 1)
        swap = ones_where(c == (r & 31) * 8 + (r >> 5))
        for g in range(PAIRS // 32):
            both = jnp.concatenate([rows_of(recv, kind, 256 * g, 256) for kind in range(2)], axis=1)
            mixed = dot(swap, both).astype(BF)
            for b in range(8):
                wide_q[32 * g : 32 * g + 32, 128 * b : 128 * b + 128] = mixed[32 * b : 32 * b + 32, :128]
                wide_p[32 * g : 32 * g + 32, 128 * b : 128 * b + 128] = mixed[32 * b : 32 * b + 32, 128:]
        hot = ones_where(iota((PAIRS, PAIRS), 0) == passage[...])
        picked = lax.dot_general(hot, wide_p[...], (((0,), (0,)), ((), ())), preferred_element_type=F32)
        summed = (wide_q[...].astype(F32) + picked).astype(BF)
        for i in range(NX):
            at = pl.multiple_of(((i - x) & 3) * ROWS, 32)
            pair[pl.ds(at, ROWS), :] = summed[ROWS * i : ROWS * i + ROWS, :]
        products(pair, copies, held, ((1, (l1, l2)), (2, (r2, r3))))

    return call(
        kernel,
        [array(PAIRS, G)] + [array(ROWS, K // 2)] * 4,
        2_500_000_000,
        12_000_000,
        vmem=44,
        in_specs=[WHOLE, WHOLE, HBM],
        scratch_shapes=[pltpu.VMEM((PAIRS, G), BF)] * 2 + HELD,
    )(recv, passage_of.reshape(1, PAIRS), proj)


def product_near(pair, proj):
    def kernel(pair, proj, l3, l0, r0, r1, turned, held, sems):
        copies = fetch(proj, held, sems)
        turned[:ROWS, :] = pair[3 * ROWS :, :]
        turned[ROWS:, :] = pair[: 3 * ROWS, :]
        products(turned, copies, held, ((0, (l3, l0)), (1, (r0, r1))))

    return call(
        kernel,
        [array(ROWS, K // 2)] * 4,
        1_700_000_000,
        10_000_000,
        vmem=44,
        in_specs=[WHOLE, HBM],
        scratch_shapes=[pltpu.VMEM((PAIRS, G), BF)] + HELD,
    )(pair, proj)


def add(a, b):
    return (a.astype(F32) + b.astype(F32)).astype(BF)


def shift(x, axis, size, by):
    return lax.ppermute(x, axis, [(i, (i + by) % size) for i in range(size)])


def across_x(recv, passage_of, proj):
    pair, l1, l2, r2, r3 = product_far(recv, passage_of, proj)
    far_l = shift(l2, "px", NX, 1)
    far_r = shift(r2, "px", NX, -1)
    l3, l0, r0, r1 = product_near(pair, proj)
    got_l = shift(l3, "px", NX, -1)
    got_r = shift(r1, "px", NX, 1)
    sum_l = shift(add(l1, far_l), "px", NX, 1)
    sum_r = shift(add(r3, far_r), "px", NX, -1)
    return sum_l, sum_r, got_l, got_r, l0, r0


def across_z(terms):
    def kernel(l2, r2, l1, r1, l0, r0, far_up, far_down, own, up1, up2, down1, down2):
        left = (l0[...].astype(F32) + l1[...].astype(F32) + l2[...].astype(F32)).astype(BF)
        right = (r0[...].astype(F32) + r1[...].astype(F32) + r2[...].astype(F32)).astype(BF)
        stacked = jnp.concatenate([left[:, :KV], left[:, KV:], right[:, :KV], right[:, KV:]], axis=0)
        r, c = iota((4 * ROWS, 4 * ROWS), 0), iota((4 * ROWS, 4 * ROWS), 1)
        block = r // 48
        quarter = (r - block * 48) // MINE
        item = r - block * 48 - quarter * MINE
        z = (block + lax.axis_index("pz")) & (NZ - 1)
        hot = ones_where(c == quarter * ROWS + z * MINE + item)
        rows = dot(hot, stacked).astype(BF)
        for k, out in ((0, own), (1, up1), (2, up2), (6, down2), (7, down1)):
            out[...] = rows[48 * k : 48 * k + 48, :]
        half = KV // 2
        far_up[0] = rows[48 * 3 : 48 * 4, :half]
        far_up[1] = rows[48 * 3 : 48 * 4, half:]
        far_up[2] = rows[48 * 4 : 48 * 5, :half]
        far_down[0] = rows[48 * 5 : 48 * 6, :half]
        far_down[1] = rows[48 * 5 : 48 * 6, half:]
        far_down[2] = rows[48 * 4 : 48 * 5, half:]

    outs = [array(3, 48, KV // 2)] * 2 + [array(48, KV)] * 5
    far_up, far_down, *near = call(kernel, outs, 300_000_000, 4_000_000)(*terms)
    far_up = shift(far_up, "pz", NZ, 2)
    far_down = shift(far_down, "pz", NZ, -2)

    def add_kernel(far_up, far_down, up1, up2, down1, down2, *outs):
        half = KV // 2
        for far, near1, near2, out1, out2, side in (
            (far_up, up1, up2, outs[0], outs[1], 0),
            (far_down, down1, down2, outs[2], outs[3], 1),
        ):
            out1[:, :half] = add(near1[:, :half], far[0])
            out1[:, half:] = add(near1[:, half:], far[1])
            for i in range(2):
                at = slice(half * i, half * i + half)
                out2[:, at] = add(near2[:, at], far[2]) if i == side else near2[:, at]

    own, *near = near
    up1, up2, down1, down2 = call(add_kernel, [array(48, KV)] * 4, 1_000_000, 1_000_000)(far_up, far_down, *near)
    up2 = shift(up2, "pz", NZ, 2)
    down2 = shift(down2, "pz", NZ, -2)
    up1 = shift(up1, "pz", NZ, 1)
    down1 = shift(down1, "pz", NZ, -1)
    return own, up2, down2, up1, down1


def last_sum(parts):
    def kernel(*refs):
        *terms, out = refs
        total = terms[0][...].astype(F32)
        for term in terms[1:]:
            total = total + term[...].astype(F32)
        for q in range(4):
            out[:, KV * q : KV * q + KV] = total[MINE * q : MINE * q + MINE, :]

    return call(kernel, array(MINE, K, dtype=F32), 1_000_000, 1_000_000)(*parts)


def local(q_fact, p_fact, q_cot, p_cot, passage_of, projection):
    recv = lax.all_to_all(grads(q_fact, p_fact, q_cot, p_cot), ("px", "pz"), 0, 0, tiled=True)
    return last_sum(across_z(across_x(recv, passage_of, permuted(projection))))


def solution(mesh):
    cut = Mesh(mesh.devices.reshape(mesh.shape["pairs"], NX, NZ), ("pairs", "px", "pz"))
    rows = P(("pairs", "px", "pz"), None)
    return jax.shard_map(
        local,
        mesh=cut,
        in_specs=(rows, rows, rows, rows, P("pairs"), P(("px", "pz"), None)),
        out_specs=rows,
        check_vma=False,
    )
```

```python
import jax
import jax.numpy as jnp
from jax import lax
from jax.experimental import pallas as pl
from jax.experimental.pallas import tpu as pltpu
from jax.sharding import Mesh, PartitionSpec as P

KV = 1024
R = 16
QLEN = 32
PLEN = 48
K = 4096
NX, NZ = 4, 8
N = NX * NZ
MINE = 12
PAIRS = N * MINE
G = 1024
ROWS = MINE * 8
MIB = 1024 * 1024
BF = jnp.bfloat16
F32 = jnp.float32
HBM = pl.BlockSpec(memory_space=pltpu.HBM)
WHOLE = pl.BlockSpec(memory_space=pltpu.VMEM)


def iota(shape, dim):
    return lax.broadcasted_iota(jnp.int32, shape, dim)


def dot(a, b):
    return lax.dot_general(a, b, (((1,), (0,)), ((), ())), preferred_element_type=F32)


def ones_where(mask):
    return jnp.where(mask, 1.0, 0.0).astype(BF)


def call(kernel, out_shape, flops, moved, vmem=24, **kwargs):
    return pl.pallas_call(
        kernel,
        out_shape=out_shape,
        compiler_params=pltpu.CompilerParams(vmem_limit_bytes=vmem * MIB),
        cost_estimate=pl.CostEstimate(flops=flops, bytes_accessed=moved, transcendentals=0),
        **kwargs,
    )


def array(*shape, dtype=BF):
    return jax.ShapeDtypeStruct(shape, dtype)


def grads(q_fact, p_fact, q_cot, p_cot):
    steps = 2
    cols = 2 * KV // steps

    def kernel(q_fact, p_fact, q_cot, p_cot, out, q_spread, p_spread):
        step = pl.program_id(0)
        lane = iota((ROWS, 128), 1)
        for kind, (fact, cot, length, spread) in enumerate(
            ((q_fact, q_cot, QLEN, q_spread), (p_fact, p_cot, PLEN, p_spread))
        ):
            tokens = MINE * length

            @pl.when(step % (steps // 2) == 0)
            def _():
                row = iota((2 * ROWS, 2 * R), 0)
                rank = jnp.where(row >= ROWS, 8, 0) + (row & 7) + (step // (steps // 2)) * R
                pick = ones_where(iota((2 * ROWS, 2 * R), 1) == rank)
                row = iota((2 * ROWS, tokens), 0)
                item = jnp.where(row >= ROWS, row - ROWS, row) >> 3
                token = iota((2 * ROWS, tokens), 1) - item * length
                held = (token >= 0) & (token < length)
                spread[...] = jnp.where(held, dot(pick, fact[...]), 0.0).astype(BF)

            grad = dot(spread[...], cot[...])
            for j in range(cols // 128):
                top = grad[:ROWS, 128 * j : 128 * j + 128]
                low = grad[ROWS:, 128 * j : 128 * j + 128]
                at = pl.ds(kind * ROWS, ROWS)
                out[2 * j, at, :] = jnp.where(lane < 64, top, pltpu.roll(low, 64, 1)).astype(BF)
                out[2 * j + 1, at, :] = jnp.where(lane < 64, pltpu.roll(top, 64, 1), low).astype(BF)

    return call(
        kernel,
        array(N, 2 * ROWS, 128),
        800_000_000,
        5_500_000,
        vmem=60,
        grid=(steps,),
        in_specs=[
            pl.BlockSpec((2 * R, MINE * QLEN), lambda n: (0, 0)),
            pl.BlockSpec((2 * R, MINE * PLEN), lambda n: (0, 0)),
            pl.BlockSpec((MINE * QLEN, cols), lambda n: (0, n)),
            pl.BlockSpec((MINE * PLEN, cols), lambda n: (0, n)),
        ],
        out_specs=pl.BlockSpec((N // steps, 2 * ROWS, 128), lambda n: (n, 0, 0)),
        scratch_shapes=[pltpu.VMEM((2 * ROWS, MINE * QLEN), BF), pltpu.VMEM((2 * ROWS, MINE * PLEN), BF)],
    )(q_fact.T, p_fact.T, q_cot, p_cot)


def permuted(projection):
    steps = 4
    cols = K // steps

    def kernel(proj, out, held, made, order, in_sems, out_sems):
        def load(n):
            return pltpu.make_async_copy(proj.at[:, pl.ds(cols * n, cols)], held.at[n], in_sems.at[n])

        def store(n):
            return pltpu.make_async_copy(made.at[n], out.at[n], out_sems.at[n])

        for n in range(steps):
            load(n).start()
        u, v = iota((G, G), 0), iota((G, G), 1)
        order[...] = ones_where(v == (u & 63) * 16 + ((u >> 6) & 1) * 8 + (u >> 7))
        for n in range(steps):
            load(n).wait()
            made[n] = dot(order[...], held[n]).astype(BF)
            store(n).start()
        for n in range(steps):
            store(n).wait()

    return call(
        kernel,
        array(12, G, KV),
        2 * G * G * K,
        16_000_000,
        vmem=57,
        in_specs=[HBM],
        out_specs=HBM,
        scratch_shapes=[
            pltpu.VMEM((steps, G, cols), BF),
            pltpu.VMEM((steps, G, cols), BF),
            pltpu.VMEM((G, G), BF),
            pltpu.SemaphoreType.DMA((steps,)),
            pltpu.SemaphoreType.DMA((steps,)),
        ],
    )(projection)


def rows_of(recv, kind, at, count):
    pieces = []
    while count:
        src, off = at // ROWS, at % ROWS
        take = min(ROWS - off, count)
        pieces.append(recv[src, kind * ROWS + off : kind * ROWS + off + take, :])
        at, count = at + take, count - take
    return jnp.concatenate(pieces, axis=0)


def fetch(proj, held, sems):
    copies = []
    for n in range(4):
        copies.append(pltpu.make_async_copy(proj.at[n], held.at[n], sems.at[n]))
        copies[n].start()
    return copies


def products(pair, copies, held, takes):
    for n in range(4):
        copies[n].wait()
        first, outs = takes[n // 2]
        part = dot(pair[ROWS * first : ROWS * (first + len(outs)), :], held[n]).astype(BF)
        at = KV * (n % 2)
        for d, out in enumerate(outs):
            out[:, at : at + KV] = part[ROWS * d : ROWS * d + ROWS, :]


HELD = [pltpu.VMEM((4, G, KV), BF), pltpu.SemaphoreType.DMA((4,))]


def product_far(recv, passage_of, proj):
    def kernel(recv, passage, proj, pair, l1, l2, r2, r3, wide_q, wide_p, held, sems):
        copies = fetch(proj, held, sems)
        x = lax.axis_index("px")
        r, c = iota((256, 256), 0), iota((256, 256), 1)
        swap = ones_where(c == (r & 31) * 8 + (r >> 5))
        for g in range(PAIRS // 32):
            both = jnp.concatenate([rows_of(recv, kind, 256 * g, 256) for kind in range(2)], axis=1)
            mixed = dot(swap, both).astype(BF)
            for b in range(8):
                wide_q[32 * g : 32 * g + 32, 128 * b : 128 * b + 128] = mixed[32 * b : 32 * b + 32, :128]
                wide_p[32 * g : 32 * g + 32, 128 * b : 128 * b + 128] = mixed[32 * b : 32 * b + 32, 128:]
        hot = ones_where(iota((PAIRS, PAIRS), 0) == passage[...])
        picked = lax.dot_general(hot, wide_p[...], (((0,), (0,)), ((), ())), preferred_element_type=F32)
        summed = (wide_q[...].astype(F32) + picked).astype(BF)
        for i in range(NX):
            at = pl.multiple_of(((i - x) & 3) * ROWS, 32)
            pair[pl.ds(at, ROWS), :] = summed[ROWS * i : ROWS * i + ROWS, :]
        products(pair, copies, held, ((1, (l1, l2)), (2, (r2, r3))))

    return call(
        kernel,
        [array(PAIRS, G)] + [array(ROWS, K // 2)] * 4,
        2_500_000_000,
        12_000_000,
        vmem=44,
        in_specs=[WHOLE, WHOLE, HBM],
        scratch_shapes=[pltpu.VMEM((PAIRS, G), BF)] * 2 + HELD,
    )(recv, passage_of.reshape(1, PAIRS), proj)


def product_near(pair, proj):
    def kernel(pair, proj, l3, l0, r0, r1, turned, held, sems):
        copies = fetch(proj, held, sems)
        turned[:ROWS, :] = pair[3 * ROWS :, :]
        turned[ROWS:, :] = pair[: 3 * ROWS, :]
        products(turned, copies, held, ((0, (l3, l0)), (1, (r0, r1))))

    return call(
        kernel,
        [array(ROWS, K // 2)] * 4,
        1_700_000_000,
        10_000_000,
        vmem=44,
        in_specs=[WHOLE, HBM],
        scratch_shapes=[pltpu.VMEM((PAIRS, G), BF)] + HELD,
    )(pair, proj)


def add(a, b):
    return (a.astype(F32) + b.astype(F32)).astype(BF)


def shift(x, axis, size, by):
    return lax.ppermute(x, axis, [(i, (i + by) % size) for i in range(size)])


def across_x(recv, passage_of, proj):
    pair, l1, l2, r2, r3 = product_far(recv, passage_of, proj)
    far_l = shift(l2, "px", NX, 1)
    far_r = shift(r2, "px", NX, -1)
    l3, l0, r0, r1 = product_near(pair, proj)
    got_l = shift(l3, "px", NX, -1)
    got_r = shift(r1, "px", NX, 1)
    sum_l = shift(add(l1, far_l), "px", NX, 1)
    sum_r = shift(add(r3, far_r), "px", NX, -1)
    return sum_l, sum_r, got_l, got_r, l0, r0


def across_z(terms):
    def kernel(l2, r2, l1, r1, l0, r0, odd_up, odd_down, own, up, down, across):
        left = (l0[...].astype(F32) + l1[...].astype(F32) + l2[...].astype(F32)).astype(BF)
        right = (r0[...].astype(F32) + r1[...].astype(F32) + r2[...].astype(F32)).astype(BF)
        stacked = jnp.concatenate([left[:, :KV], left[:, KV:], right[:, :KV], right[:, KV:]], axis=0)
        r, c = iota((4 * ROWS, 4 * ROWS), 0), iota((4 * ROWS, 4 * ROWS), 1)
        block = r // 48
        quarter = (r - block * 48) // MINE
        item = r - block * 48 - quarter * MINE
        z = (block + lax.axis_index("pz")) & (NZ - 1)
        hot = ones_where(c == quarter * ROWS + z * MINE + item)
        rows = dot(hot, stacked).astype(BF)
        outs = (own, odd_up.at[0], up, odd_up.at[1], across, odd_down.at[1], down, odd_down.at[0])
        for k, out in enumerate(outs):
            out[...] = rows[48 * k : 48 * k + 48, :]

    outs = [array(2, 48, KV)] * 2 + [array(48, KV)] * 4
    odd_up, odd_down, own, up, down, across = call(kernel, outs, 300_000_000, 4_000_000)(*terms)
    odd_up = shift(odd_up, "pz", NZ, 1)
    odd_down = shift(odd_down, "pz", NZ, -1)
    across = shift(across, "pz", NZ, 4)
    up = shift(add(up, odd_up[1]), "pz", NZ, 2)
    down = shift(add(down, odd_down[1]), "pz", NZ, -2)
    return up, down, odd_up, odd_down, across, own


def last_sum(parts):
    def kernel(up, down, odd_up, odd_down, across, own, out):
        total = own[...].astype(F32)
        for term in (odd_up[0], odd_down[0], across[...], up[...], down[...]):
            total = total + term.astype(F32)
        for q in range(4):
            out[:, KV * q : KV * q + KV] = total[MINE * q : MINE * q + MINE, :]

    return call(kernel, array(MINE, K, dtype=F32), 1_000_000, 1_000_000)(*parts)


def local(q_fact, p_fact, q_cot, p_cot, passage_of, projection):
    recv = lax.all_to_all(grads(q_fact, p_fact, q_cot, p_cot), ("px", "pz"), 0, 0, tiled=True)
    return last_sum(across_z(across_x(recv, passage_of, permuted(projection))))


def solution(mesh):
    cut = Mesh(mesh.devices.reshape(mesh.shape["pairs"], NX, NZ), ("pairs", "px", "pz"))
    rows = P(("pairs", "px", "pz"), None)
    return jax.shard_map(
        local,
        mesh=cut,
        in_specs=(rows, rows, rows, rows, P("pairs"), P(("px", "pz"), None)),
        out_specs=rows,
        check_vma=False,
    )
```

```python
import jax
import jax.numpy as jnp
from jax import lax
from jax.experimental import pallas as pl
from jax.experimental.pallas import tpu as pltpu
from jax.sharding import Mesh, PartitionSpec as P

KV = 1024
R = 16
QLEN = 32
PLEN = 48
K = 4096
NX, NZ = 4, 8
N = NX * NZ
MINE = 12
PAIRS = N * MINE
G = 1024
ROWS = MINE * 8
MIB = 1024 * 1024
BF = jnp.bfloat16
F32 = jnp.float32
HBM = pl.BlockSpec(memory_space=pltpu.HBM)
WHOLE = pl.BlockSpec(memory_space=pltpu.VMEM)


def iota(shape, dim):
    return lax.broadcasted_iota(jnp.int32, shape, dim)


def dot(a, b):
    return lax.dot_general(a, b, (((1,), (0,)), ((), ())), preferred_element_type=F32)


def ones_where(mask):
    return jnp.where(mask, 1.0, 0.0).astype(BF)


def call(kernel, out_shape, flops, moved, vmem=24, **kwargs):
    return pl.pallas_call(
        kernel,
        out_shape=out_shape,
        compiler_params=pltpu.CompilerParams(vmem_limit_bytes=vmem * MIB),
        cost_estimate=pl.CostEstimate(flops=flops, bytes_accessed=moved, transcendentals=0),
        **kwargs,
    )


def array(*shape, dtype=BF):
    return jax.ShapeDtypeStruct(shape, dtype)


def grads(q_fact, p_fact, q_cot, p_cot):
    steps = 2
    cols = 2 * KV // steps

    def kernel(q_fact, p_fact, q_cot, p_cot, out, q_spread, p_spread):
        step = pl.program_id(0)
        lane = iota((ROWS, 128), 1)
        for kind, (fact, cot, length, spread) in enumerate(
            ((q_fact, q_cot, QLEN, q_spread), (p_fact, p_cot, PLEN, p_spread))
        ):
            tokens = MINE * length

            @pl.when(step % (steps // 2) == 0)
            def _():
                row = iota((2 * ROWS, 2 * R), 0)
                rank = jnp.where(row >= ROWS, 8, 0) + (row & 7) + (step // (steps // 2)) * R
                pick = ones_where(iota((2 * ROWS, 2 * R), 1) == rank)
                row = iota((2 * ROWS, tokens), 0)
                item = jnp.where(row >= ROWS, row - ROWS, row) >> 3
                token = iota((2 * ROWS, tokens), 1) - item * length
                held = (token >= 0) & (token < length)
                spread[...] = jnp.where(held, dot(pick, fact[...]), 0.0).astype(BF)

            grad = dot(spread[...], cot[...])
            for j in range(cols // 128):
                top = grad[:ROWS, 128 * j : 128 * j + 128]
                low = grad[ROWS:, 128 * j : 128 * j + 128]
                at = pl.ds(kind * ROWS, ROWS)
                out[2 * j, at, :] = jnp.where(lane < 64, top, pltpu.roll(low, 64, 1)).astype(BF)
                out[2 * j + 1, at, :] = jnp.where(lane < 64, pltpu.roll(top, 64, 1), low).astype(BF)

    return call(
        kernel,
        array(N, 2 * ROWS, 128),
        800_000_000,
        5_500_000,
        vmem=60,
        grid=(steps,),
        in_specs=[
            pl.BlockSpec((2 * R, MINE * QLEN), lambda n: (0, 0)),
            pl.BlockSpec((2 * R, MINE * PLEN), lambda n: (0, 0)),
            pl.BlockSpec((MINE * QLEN, cols), lambda n: (0, n)),
            pl.BlockSpec((MINE * PLEN, cols), lambda n: (0, n)),
        ],
        out_specs=pl.BlockSpec((N // steps, 2 * ROWS, 128), lambda n: (n, 0, 0)),
        scratch_shapes=[pltpu.VMEM((2 * ROWS, MINE * QLEN), BF), pltpu.VMEM((2 * ROWS, MINE * PLEN), BF)],
    )(q_fact.T, p_fact.T, q_cot, p_cot)


def permuted(projection):
    steps = 4
    cols = K // steps

    def kernel(proj, out, held, made, order, in_sems, out_sems):
        def load(n):
            return pltpu.make_async_copy(proj.at[:, pl.ds(cols * n, cols)], held.at[n], in_sems.at[n])

        def store(n):
            return pltpu.make_async_copy(made.at[n], out.at[n], out_sems.at[n])

        for n in range(steps):
            load(n).start()
        u, v = iota((G, G), 0), iota((G, G), 1)
        order[...] = ones_where(v == (u & 63) * 16 + ((u >> 6) & 1) * 8 + (u >> 7))
        for n in range(steps):
            load(n).wait()
            made[n] = dot(order[...], held[n]).astype(BF)
            store(n).start()
        for n in range(steps):
            store(n).wait()

    return call(
        kernel,
        array(12, G, KV),
        2 * G * G * K,
        16_000_000,
        vmem=57,
        in_specs=[HBM],
        out_specs=HBM,
        scratch_shapes=[
            pltpu.VMEM((steps, G, cols), BF),
            pltpu.VMEM((steps, G, cols), BF),
            pltpu.VMEM((G, G), BF),
            pltpu.SemaphoreType.DMA((steps,)),
            pltpu.SemaphoreType.DMA((steps,)),
        ],
    )(projection)


def rows_of(recv, kind, at, count):
    pieces = []
    while count:
        src, off = at // ROWS, at % ROWS
        take = min(ROWS - off, count)
        pieces.append(recv[src, kind * ROWS + off : kind * ROWS + off + take, :])
        at, count = at + take, count - take
    return jnp.concatenate(pieces, axis=0)


def fetch(proj, held, sems):
    copies = []
    for n in range(4):
        copies.append(pltpu.make_async_copy(proj.at[n], held.at[n], sems.at[n]))
        copies[n].start()
    return copies


def products(pair, copies, held, takes):
    for n in range(4):
        copies[n].wait()
        first, outs = takes[n // 2]
        part = dot(pair[ROWS * first : ROWS * (first + len(outs)), :], held[n]).astype(BF)
        at = KV * (n % 2)
        for d, out in enumerate(outs):
            out[:, at : at + KV] = part[ROWS * d : ROWS * d + ROWS, :]


HELD = [pltpu.VMEM((4, G, KV), BF), pltpu.SemaphoreType.DMA((4,))]


def product_far(recv, passage_of, proj):
    def kernel(recv, passage, proj, pair, l1, l2, r2, r3, wide_q, wide_p, held, sems):
        copies = fetch(proj, held, sems)
        x = lax.axis_index("px")
        r, c = iota((256, 256), 0), iota((256, 256), 1)
        swap = ones_where(c == (r & 31) * 8 + (r >> 5))
        for g in range(PAIRS // 32):
            both = jnp.concatenate([rows_of(recv, kind, 256 * g, 256) for kind in range(2)], axis=1)
            mixed = dot(swap, both).astype(BF)
            for b in range(8):
                wide_q[32 * g : 32 * g + 32, 128 * b : 128 * b + 128] = mixed[32 * b : 32 * b + 32, :128]
                wide_p[32 * g : 32 * g + 32, 128 * b : 128 * b + 128] = mixed[32 * b : 32 * b + 32, 128:]
        hot = ones_where(iota((PAIRS, PAIRS), 0) == passage[...])
        picked = lax.dot_general(hot, wide_p[...], (((0,), (0,)), ((), ())), preferred_element_type=F32)
        summed = (wide_q[...].astype(F32) + picked).astype(BF)
        for i in range(NX):
            at = pl.multiple_of(((i - x) & 3) * ROWS, 32)
            pair[pl.ds(at, ROWS), :] = summed[ROWS * i : ROWS * i + ROWS, :]
        products(pair, copies, held, ((1, (l1, l2)), (2, (r2, r3))))

    return call(
        kernel,
        [array(PAIRS, G)] + [array(ROWS, K // 2)] * 4,
        2_500_000_000,
        12_000_000,
        vmem=44,
        in_specs=[WHOLE, WHOLE, HBM],
        scratch_shapes=[pltpu.VMEM((PAIRS, G), BF)] * 2 + HELD,
    )(recv, passage_of.reshape(1, PAIRS), proj)


def product_near(pair, proj):
    def kernel(pair, proj, l3, l0, r0, r1, turned, held, sems):
        copies = fetch(proj, held, sems)
        turned[:ROWS, :] = pair[3 * ROWS :, :]
        turned[ROWS:, :] = pair[: 3 * ROWS, :]
        products(turned, copies, held, ((0, (l3, l0)), (1, (r0, r1))))

    return call(
        kernel,
        [array(ROWS, K // 2)] * 4,
        1_700_000_000,
        10_000_000,
        vmem=44,
        in_specs=[WHOLE, HBM],
        scratch_shapes=[pltpu.VMEM((PAIRS, G), BF)] + HELD,
    )(pair, proj)


def add(a, b):
    return (a.astype(F32) + b.astype(F32)).astype(BF)


def shift(x, axis, size, by):
    return lax.ppermute(x, axis, [(i, (i + by) % size) for i in range(size)])


def across_x(recv, passage_of, proj):
    pair, l1, l2, r2, r3 = product_far(recv, passage_of, proj)
    far_l = shift(l2, "px", NX, 1)
    far_r = shift(r2, "px", NX, -1)
    l3, l0, r0, r1 = product_near(pair, proj)
    got_l = shift(l3, "px", NX, -1)
    got_r = shift(r1, "px", NX, 1)
    sum_l = shift(add(l1, far_l), "px", NX, 1)
    sum_r = shift(add(r3, far_r), "px", NX, -1)
    return sum_l, sum_r, got_l, got_r, l0, r0


def across_z(terms):
    def kernel(l2, r2, l1, r1, l0, r0, odd_up, odd_down, own, up, down, across):
        left = (l0[...].astype(F32) + l1[...].astype(F32) + l2[...].astype(F32)).astype(BF)
        right = (r0[...].astype(F32) + r1[...].astype(F32) + r2[...].astype(F32)).astype(BF)
        stacked = jnp.concatenate([left[:, :KV], left[:, KV:], right[:, :KV], right[:, KV:]], axis=0)
        r, c = iota((4 * ROWS, 4 * ROWS), 0), iota((4 * ROWS, 4 * ROWS), 1)
        block = r // 48
        quarter = (r - block * 48) // MINE
        item = r - block * 48 - quarter * MINE
        z = (block + lax.axis_index("pz")) & (NZ - 1)
        hot = ones_where(c == quarter * ROWS + z * MINE + item)
        rows = dot(hot, stacked).astype(BF)
        outs = (own, odd_up.at[0], up, odd_up.at[1], across, odd_down.at[1], down, odd_down.at[0])
        for k, out in enumerate(outs):
            out[...] = rows[48 * k : 48 * k + 48, :]

    outs = [array(2, 48, KV)] * 2 + [array(48, KV)] * 4
    odd_up, odd_down, own, up, down, across = call(kernel, outs, 300_000_000, 4_000_000)(*terms)
    odd_up = shift(odd_up, "pz", NZ, 1)
    odd_down = shift(odd_down, "pz", NZ, -1)
    across = shift(across, "pz", NZ, 4)
    odd_up, odd_down = lax.optimization_barrier((odd_up, odd_down))
    up = shift(add(up, odd_up[1]), "pz", NZ, 2)
    down = shift(add(down, odd_down[1]), "pz", NZ, -2)
    return up, down, odd_up, odd_down, across, own


def last_sum(parts):
    def kernel(up, down, odd_up, odd_down, across, own, out):
        total = own[...].astype(F32)
        for term in (odd_up[0], odd_down[0], across[...], up[...], down[...]):
            total = total + term.astype(F32)
        for q in range(4):
            out[:, KV * q : KV * q + KV] = total[MINE * q : MINE * q + MINE, :]

    return call(kernel, array(MINE, K, dtype=F32), 1_000_000, 1_000_000)(*parts)


def local(q_fact, p_fact, q_cot, p_cot, passage_of, projection):
    recv = lax.all_to_all(grads(q_fact, p_fact, q_cot, p_cot), ("px", "pz"), 0, 0, tiled=True)
    return last_sum(across_z(across_x(recv, passage_of, permuted(projection))))


def solution(mesh):
    cut = Mesh(mesh.devices.reshape(mesh.shape["pairs"], NX, NZ), ("pairs", "px", "pz"))
    rows = P(("pairs", "px", "pz"), None)
    return jax.shard_map(
        local,
        mesh=cut,
        in_specs=(rows, rows, rows, rows, P("pairs"), P(("px", "pz"), None)),
        out_specs=rows,
        check_vma=False,
    )
```

```python
import jax
import jax.numpy as jnp
from jax import lax
from jax.experimental import pallas as pl
from jax.experimental.pallas import tpu as pltpu
from jax.sharding import Mesh, PartitionSpec as P

KV = 1024
R = 16
QLEN = 32
PLEN = 48
K = 4096
NX, NZ = 4, 8
N = NX * NZ
MINE = 12
PAIRS = N * MINE
G = 1024
ROWS = MINE * 8
MIB = 1024 * 1024
BF = jnp.bfloat16
F32 = jnp.float32
HBM = pl.BlockSpec(memory_space=pltpu.HBM)
WHOLE = pl.BlockSpec(memory_space=pltpu.VMEM)


def iota(shape, dim):
    return lax.broadcasted_iota(jnp.int32, shape, dim)


def dot(a, b):
    return lax.dot_general(a, b, (((1,), (0,)), ((), ())), preferred_element_type=F32)


def ones_where(mask):
    return jnp.where(mask, 1.0, 0.0).astype(BF)


def call(kernel, out_shape, flops, moved, vmem=24, **kwargs):
    return pl.pallas_call(
        kernel,
        out_shape=out_shape,
        compiler_params=pltpu.CompilerParams(vmem_limit_bytes=vmem * MIB),
        cost_estimate=pl.CostEstimate(flops=flops, bytes_accessed=moved, transcendentals=0),
        **kwargs,
    )


def array(*shape, dtype=BF):
    return jax.ShapeDtypeStruct(shape, dtype)


def grads(q_fact, p_fact, q_cot, p_cot):
    steps = 2
    cols = 2 * KV // steps

    def kernel(q_fact, p_fact, q_cot, p_cot, out, q_spread, p_spread):
        step = pl.program_id(0)
        lane = iota((ROWS, 128), 1)
        for kind, (fact, cot, length, spread) in enumerate(
            ((q_fact, q_cot, QLEN, q_spread), (p_fact, p_cot, PLEN, p_spread))
        ):
            tokens = MINE * length

            @pl.when(step % (steps // 2) == 0)
            def _():
                row = iota((2 * ROWS, 2 * R), 0)
                rank = jnp.where(row >= ROWS, 8, 0) + (row & 7) + (step // (steps // 2)) * R
                pick = ones_where(iota((2 * ROWS, 2 * R), 1) == rank)
                row = iota((2 * ROWS, tokens), 0)
                item = jnp.where(row >= ROWS, row - ROWS, row) >> 3
                token = iota((2 * ROWS, tokens), 1) - item * length
                held = (token >= 0) & (token < length)
                spread[...] = jnp.where(held, dot(pick, fact[...]), 0.0).astype(BF)

            grad = dot(spread[...], cot[...])
            for j in range(cols // 128):
                top = grad[:ROWS, 128 * j : 128 * j + 128]
                low = grad[ROWS:, 128 * j : 128 * j + 128]
                at = pl.ds(kind * ROWS, ROWS)
                out[2 * j, at, :] = jnp.where(lane < 64, top, pltpu.roll(low, 64, 1)).astype(BF)
                out[2 * j + 1, at, :] = jnp.where(lane < 64, pltpu.roll(top, 64, 1), low).astype(BF)

    return call(
        kernel,
        array(N, 2 * ROWS, 128),
        800_000_000,
        5_500_000,
        vmem=60,
        grid=(steps,),
        in_specs=[
            pl.BlockSpec((2 * R, MINE * QLEN), lambda n: (0, 0)),
            pl.BlockSpec((2 * R, MINE * PLEN), lambda n: (0, 0)),
            pl.BlockSpec((MINE * QLEN, cols), lambda n: (0, n)),
            pl.BlockSpec((MINE * PLEN, cols), lambda n: (0, n)),
        ],
        out_specs=pl.BlockSpec((N // steps, 2 * ROWS, 128), lambda n: (n, 0, 0)),
        scratch_shapes=[pltpu.VMEM((2 * ROWS, MINE * QLEN), BF), pltpu.VMEM((2 * ROWS, MINE * PLEN), BF)],
    )(q_fact.T, p_fact.T, q_cot, p_cot)


def permuted(projection):
    steps = 4
    cols = K // steps

    def kernel(proj, out, held, made, order, in_sems, out_sems):
        def load(n):
            return pltpu.make_async_copy(proj.at[:, pl.ds(cols * n, cols)], held.at[n], in_sems.at[n])

        def store(n):
            return pltpu.make_async_copy(made.at[n], out.at[n], out_sems.at[n])

        for n in range(steps):
            load(n).start()
        u, v = iota((G, G), 0), iota((G, G), 1)
        order[...] = ones_where(v == (u & 63) * 16 + ((u >> 6) & 1) * 8 + (u >> 7))
        for n in range(steps):
            load(n).wait()
            made[n] = dot(order[...], held[n]).astype(BF)
            store(n).start()
        for n in range(steps):
            store(n).wait()

    return call(
        kernel,
        array(12, G, KV),
        2 * G * G * K,
        16_000_000,
        vmem=57,
        in_specs=[HBM],
        out_specs=HBM,
        scratch_shapes=[
            pltpu.VMEM((steps, G, cols), BF),
            pltpu.VMEM((steps, G, cols), BF),
            pltpu.VMEM((G, G), BF),
            pltpu.SemaphoreType.DMA((steps,)),
            pltpu.SemaphoreType.DMA((steps,)),
        ],
    )(projection)


def rows_of(recv, kind, at, count):
    pieces = []
    while count:
        src, off = at // ROWS, at % ROWS
        take = min(ROWS - off, count)
        pieces.append(recv[src, kind * ROWS + off : kind * ROWS + off + take, :])
        at, count = at + take, count - take
    return jnp.concatenate(pieces, axis=0)


def fetch(proj, held, sems):
    copies = []
    for n in range(4):
        copies.append(pltpu.make_async_copy(proj.at[n], held.at[n], sems.at[n]))
        copies[n].start()
    return copies


def products(pair, copies, held, takes):
    for n in range(4):
        copies[n].wait()
        first, outs = takes[n // 2]
        part = dot(pair[ROWS * first : ROWS * (first + len(outs)), :], held[n]).astype(BF)
        at = KV * (n % 2)
        for d, out in enumerate(outs):
            out[:, at : at + KV] = part[ROWS * d : ROWS * d + ROWS, :]


HELD = [pltpu.VMEM((4, G, KV), BF), pltpu.SemaphoreType.DMA((4,))]


def product_far(recv, passage_of, proj):
    def kernel(recv, passage, proj, pair, l1, l2, r2, r3, wide_q, wide_p, held, sems):
        copies = fetch(proj, held, sems)
        x = lax.axis_index("px")
        r, c = iota((256, 256), 0), iota((256, 256), 1)
        swap = ones_where(c == (r & 31) * 8 + (r >> 5))
        for g in range(PAIRS // 32):
            both = jnp.concatenate([rows_of(recv, kind, 256 * g, 256) for kind in range(2)], axis=1)
            mixed = dot(swap, both).astype(BF)
            for b in range(8):
                wide_q[32 * g : 32 * g + 32, 128 * b : 128 * b + 128] = mixed[32 * b : 32 * b + 32, :128]
                wide_p[32 * g : 32 * g + 32, 128 * b : 128 * b + 128] = mixed[32 * b : 32 * b + 32, 128:]
        hot = ones_where(iota((PAIRS, PAIRS), 0) == passage[...])
        picked = lax.dot_general(hot, wide_p[...], (((0,), (0,)), ((), ())), preferred_element_type=F32)
        summed = (wide_q[...].astype(F32) + picked).astype(BF)
        for i in range(NX):
            at = pl.multiple_of(((i - x) & 3) * ROWS, 32)
            pair[pl.ds(at, ROWS), :] = summed[ROWS * i : ROWS * i + ROWS, :]
        products(pair, copies, held, ((1, (l1, l2)), (2, (r2, r3))))

    return call(
        kernel,
        [array(PAIRS, G)] + [array(ROWS, K // 2)] * 4,
        2_500_000_000,
        12_000_000,
        vmem=44,
        in_specs=[WHOLE, WHOLE, HBM],
        scratch_shapes=[pltpu.VMEM((PAIRS, G), BF)] * 2 + HELD,
    )(recv, passage_of.reshape(1, PAIRS), proj)


def product_near(pair, proj):
    def kernel(pair, proj, l3, l0, r0, r1, turned, held, sems):
        copies = fetch(proj, held, sems)
        turned[:ROWS, :] = pair[3 * ROWS :, :]
        turned[ROWS:, :] = pair[: 3 * ROWS, :]
        products(turned, copies, held, ((0, (l3, l0)), (1, (r0, r1))))

    return call(
        kernel,
        [array(ROWS, K // 2)] * 4,
        1_700_000_000,
        10_000_000,
        vmem=44,
        in_specs=[WHOLE, HBM],
        scratch_shapes=[pltpu.VMEM((PAIRS, G), BF)] + HELD,
    )(pair, proj)


def add(a, b):
    return (a.astype(F32) + b.astype(F32)).astype(BF)


def shift(x, axis, size, by):
    return lax.ppermute(x, axis, [(i, (i + by) % size) for i in range(size)])


def across_x(recv, passage_of, proj):
    pair, l1, l2, r2, r3 = product_far(recv, passage_of, proj)
    far_l = shift(l2, "px", NX, 1)
    far_r = shift(r2, "px", NX, -1)
    l3, l0, r0, r1 = product_near(pair, proj)
    got_l = shift(l3, "px", NX, -1)
    got_r = shift(r1, "px", NX, 1)
    sum_l = shift(add(l1, far_l), "px", NX, 1)
    sum_r = shift(add(r3, far_r), "px", NX, -1)
    return sum_l, sum_r, got_l, got_r, l0, r0


def across_z(terms):
    def kernel(l2, r2, l1, r1, l0, r0, odd_up, odd_down, own, up, down, far_up, far_down):
        left = (l0[...].astype(F32) + l1[...].astype(F32) + l2[...].astype(F32)).astype(BF)
        right = (r0[...].astype(F32) + r1[...].astype(F32) + r2[...].astype(F32)).astype(BF)
        stacked = jnp.concatenate([left[:, :KV], left[:, KV:], right[:, :KV], right[:, KV:]], axis=0)
        r, c = iota((4 * ROWS, 4 * ROWS), 0), iota((4 * ROWS, 4 * ROWS), 1)
        block = r // 48
        quarter = (r - block * 48) // MINE
        item = r - block * 48 - quarter * MINE
        z = (block + lax.axis_index("pz")) & (NZ - 1)
        hot = ones_where(c == quarter * ROWS + z * MINE + item)
        rows = dot(hot, stacked).astype(BF)
        outs = (own, odd_up.at[0], up, odd_up.at[1], None, odd_down.at[1], down, odd_down.at[0])
        for k, out in enumerate(outs):
            if k != 4:
                out[...] = rows[48 * k : 48 * k + 48, :]
        far_up[...] = rows[48 * 4 : 48 * 5, : KV // 2]
        far_down[...] = rows[48 * 4 : 48 * 5, KV // 2 :]

    outs = [array(2, 48, KV)] * 2 + [array(48, KV)] * 3 + [array(48, KV // 2)] * 2
    odd_up, odd_down, own, up, down, far_up, far_down = call(kernel, outs, 300_000_000, 4_000_000)(*terms)
    odd_up = shift(odd_up, "pz", NZ, 1)
    odd_down = shift(odd_down, "pz", NZ, -1)
    far_up = shift(far_up, "pz", NZ, 2)
    far_down = shift(far_down, "pz", NZ, -2)

    def add_kernel(odd_up, odd_down, far_up, far_down, up, down, up_out, down_out):
        half = KV // 2
        for near, odd, far, out, first in ((up, odd_up, far_up, up_out, 0), (down, odd_down, far_down, down_out, half)):
            total = near[...].astype(F32) + odd[1].astype(F32)
            at, rest = slice(first, first + half), slice(half - first, KV - first)
            out[:, at] = (total[:, at] + far[...].astype(F32)).astype(BF)
            out[:, rest] = total[:, rest].astype(BF)

    inputs = (odd_up, odd_down, far_up, far_down, up, down)
    up, down = call(add_kernel, [array(48, KV)] * 2, 1_000_000, 1_000_000)(*inputs)
    up = shift(up, "pz", NZ, 2)
    down = shift(down, "pz", NZ, -2)
    return up, down, odd_up, odd_down, own


def last_sum(parts):
    def kernel(up, down, odd_up, odd_down, own, out):
        total = own[...].astype(F32)
        for term in (odd_up[0], odd_down[0], up[...], down[...]):
            total = total + term.astype(F32)
        for q in range(4):
            out[:, KV * q : KV * q + KV] = total[MINE * q : MINE * q + MINE, :]

    return call(kernel, array(MINE, K, dtype=F32), 1_000_000, 1_000_000)(*parts)


def local(q_fact, p_fact, q_cot, p_cot, passage_of, projection):
    recv = lax.all_to_all(grads(q_fact, p_fact, q_cot, p_cot), ("px", "pz"), 0, 0, tiled=True)
    return last_sum(across_z(across_x(recv, passage_of, permuted(projection))))


def solution(mesh):
    cut = Mesh(mesh.devices.reshape(mesh.shape["pairs"], NX, NZ), ("pairs", "px", "pz"))
    rows = P(("pairs", "px", "pz"), None)
    return jax.shard_map(
        local,
        mesh=cut,
        in_specs=(rows, rows, rows, rows, P("pairs"), P(("px", "pz"), None)),
        out_specs=rows,
        check_vma=False,
    )
```

```python
import jax
import jax.numpy as jnp
from jax import lax
from jax.experimental import pallas as pl
from jax.experimental.pallas import tpu as pltpu
from jax.sharding import Mesh, PartitionSpec as P

KV = 1024
R = 16
QLEN = 32
PLEN = 48
K = 4096
NX, NZ = 4, 8
N = NX * NZ
MINE = 12
PAIRS = N * MINE
G = 1024
ROWS = MINE * 8
MIB = 1024 * 1024
BF = jnp.bfloat16
F32 = jnp.float32
HBM = pl.BlockSpec(memory_space=pltpu.HBM)
WHOLE = pl.BlockSpec(memory_space=pltpu.VMEM)


def iota(shape, dim):
    return lax.broadcasted_iota(jnp.int32, shape, dim)


def dot(a, b):
    return lax.dot_general(a, b, (((1,), (0,)), ((), ())), preferred_element_type=F32)


def ones_where(mask):
    return jnp.where(mask, 1.0, 0.0).astype(BF)


def call(kernel, out_shape, flops, moved, vmem=24, **kwargs):
    return pl.pallas_call(
        kernel,
        out_shape=out_shape,
        compiler_params=pltpu.CompilerParams(vmem_limit_bytes=vmem * MIB),
        cost_estimate=pl.CostEstimate(flops=flops, bytes_accessed=moved, transcendentals=0),
        **kwargs,
    )


def array(*shape, dtype=BF):
    return jax.ShapeDtypeStruct(shape, dtype)


def grads(q_fact, p_fact, q_cot, p_cot):
    steps = 2
    cols = 2 * KV // steps

    def kernel(q_fact, p_fact, q_cot, p_cot, out, q_spread, p_spread):
        step = pl.program_id(0)
        lane = iota((ROWS, 128), 1)
        for kind, (fact, cot, length, spread) in enumerate(
            ((q_fact, q_cot, QLEN, q_spread), (p_fact, p_cot, PLEN, p_spread))
        ):
            tokens = MINE * length

            @pl.when(step % (steps // 2) == 0)
            def _():
                row = iota((2 * ROWS, 2 * R), 0)
                rank = jnp.where(row >= ROWS, 8, 0) + (row & 7) + (step // (steps // 2)) * R
                pick = ones_where(iota((2 * ROWS, 2 * R), 1) == rank)
                row = iota((2 * ROWS, tokens), 0)
                item = jnp.where(row >= ROWS, row - ROWS, row) >> 3
                token = iota((2 * ROWS, tokens), 1) - item * length
                held = (token >= 0) & (token < length)
                spread[...] = jnp.where(held, dot(pick, fact[...]), 0.0).astype(BF)

            grad = dot(spread[...], cot[...])
            for j in range(cols // 128):
                top = grad[:ROWS, 128 * j : 128 * j + 128]
                low = grad[ROWS:, 128 * j : 128 * j + 128]
                at = pl.ds(kind * ROWS, ROWS)
                out[2 * j, at, :] = jnp.where(lane < 64, top, pltpu.roll(low, 64, 1)).astype(BF)
                out[2 * j + 1, at, :] = jnp.where(lane < 64, pltpu.roll(top, 64, 1), low).astype(BF)

    return call(
        kernel,
        array(N, 2 * ROWS, 128),
        800_000_000,
        5_500_000,
        vmem=60,
        grid=(steps,),
        in_specs=[
            pl.BlockSpec((2 * R, MINE * QLEN), lambda n: (0, 0)),
            pl.BlockSpec((2 * R, MINE * PLEN), lambda n: (0, 0)),
            pl.BlockSpec((MINE * QLEN, cols), lambda n: (0, n)),
            pl.BlockSpec((MINE * PLEN, cols), lambda n: (0, n)),
        ],
        out_specs=pl.BlockSpec((N // steps, 2 * ROWS, 128), lambda n: (n, 0, 0)),
        scratch_shapes=[pltpu.VMEM((2 * ROWS, MINE * QLEN), BF), pltpu.VMEM((2 * ROWS, MINE * PLEN), BF)],
    )(q_fact.T, p_fact.T, q_cot, p_cot)


def permuted(projection):
    steps = 4
    cols = K // steps

    def kernel(proj, out, held, made, order, in_sems, out_sems):
        def load(n):
            return pltpu.make_async_copy(proj.at[:, pl.ds(cols * n, cols)], held.at[n], in_sems.at[n])

        def store(n):
            return pltpu.make_async_copy(made.at[n], out.at[n], out_sems.at[n])

        for n in range(steps):
            load(n).start()
        u, v = iota((G, G), 0), iota((G, G), 1)
        order[...] = ones_where(v == (u & 63) * 16 + ((u >> 6) & 1) * 8 + (u >> 7))
        for n in range(steps):
            load(n).wait()
            made[n] = dot(order[...], held[n]).astype(BF)
            store(n).start()
        for n in range(steps):
            store(n).wait()

    return call(
        kernel,
        array(12, G, KV),
        2 * G * G * K,
        16_000_000,
        vmem=57,
        in_specs=[HBM],
        out_specs=HBM,
        scratch_shapes=[
            pltpu.VMEM((steps, G, cols), BF),
            pltpu.VMEM((steps, G, cols), BF),
            pltpu.VMEM((G, G), BF),
            pltpu.SemaphoreType.DMA((steps,)),
            pltpu.SemaphoreType.DMA((steps,)),
        ],
    )(projection)


def rows_of(recv, kind, at, count):
    pieces = []
    while count:
        src, off = at // ROWS, at % ROWS
        take = min(ROWS - off, count)
        pieces.append(recv[src, kind * ROWS + off : kind * ROWS + off + take, :])
        at, count = at + take, count - take
    return jnp.concatenate(pieces, axis=0)


def fetch(proj, held, sems):
    copies = []
    for n in range(4):
        copies.append(pltpu.make_async_copy(proj.at[n], held.at[n], sems.at[n]))
        copies[n].start()
    return copies


def product(recv, passage_of, proj):
    def kernel(recv, passage, proj, l0, l1, l2, l3, r0, r1, r2, r3, wide_q, wide_p, pair, held, sems):
        copies = fetch(proj, held, sems)
        x = lax.axis_index("px")
        r, c = iota((256, 256), 0), iota((256, 256), 1)
        swap = ones_where(c == (r & 31) * 8 + (r >> 5))
        for g in range(PAIRS // 32):
            both = jnp.concatenate([rows_of(recv, kind, 256 * g, 256) for kind in range(2)], axis=1)
            mixed = dot(swap, both).astype(BF)
            for b in range(8):
                wide_q[32 * g : 32 * g + 32, 128 * b : 128 * b + 128] = mixed[32 * b : 32 * b + 32, :128]
                wide_p[32 * g : 32 * g + 32, 128 * b : 128 * b + 128] = mixed[32 * b : 32 * b + 32, 128:]
        hot = ones_where(iota((PAIRS, PAIRS), 0) == passage[...])
        picked = lax.dot_general(hot, wide_p[...], (((0,), (0,)), ((), ())), preferred_element_type=F32)
        summed = (wide_q[...].astype(F32) + picked).astype(BF)
        for i in range(NX):
            at = pl.multiple_of(((i - x) & 3) * ROWS, 32)
            pair[pl.ds(at, ROWS), :] = summed[ROWS * i : ROWS * i + ROWS, :]
        for n in range(4):
            copies[n].wait()
            part = dot(pair[...], held[n]).astype(BF)
            at = KV * (n % 2)
            for d, out in enumerate(((l0, l1, l2, l3), (r0, r1, r2, r3))[n // 2]):
                out[:, at : at + KV] = part[ROWS * d : ROWS * d + ROWS, :]

    return call(
        kernel,
        [array(ROWS, K // 2)] * 8,
        4_000_000_000,
        12_000_000,
        vmem=44,
        in_specs=[WHOLE, WHOLE, HBM],
        scratch_shapes=[pltpu.VMEM((PAIRS, G), BF)] * 3
        + [pltpu.VMEM((4, G, KV), BF), pltpu.SemaphoreType.DMA((4,))],
    )(recv, passage_of.reshape(1, PAIRS), proj)


def add(a, b):
    return (a.astype(F32) + b.astype(F32)).astype(BF)


def shift(x, axis, size, by):
    return lax.ppermute(x, axis, [(i, (i + by) % size) for i in range(size)])


def across_x(recv, passage_of, proj):
    l0, l1, l2, l3, r0, r1, r2, r3 = product(recv, passage_of, proj)
    far_l = shift(l2, "px", NX, 1)
    far_r = shift(r2, "px", NX, -1)
    got_l = shift(l3, "px", NX, -1)
    got_r = shift(r1, "px", NX, 1)
    sum_l = shift(add(l1, far_l), "px", NX, 1)
    sum_r = shift(add(r3, far_r), "px", NX, -1)
    return sum_l, sum_r, got_l, got_r, l0, r0


def across_z(terms):
    def kernel(l2, r2, l1, r1, l0, r0, odd_up, odd_down, own, up, down, far_up, far_down):
        left = (l0[...].astype(F32) + l1[...].astype(F32) + l2[...].astype(F32)).astype(BF)
        right = (r0[...].astype(F32) + r1[...].astype(F32) + r2[...].astype(F32)).astype(BF)
        stacked = jnp.concatenate([left[:, :KV], left[:, KV:], right[:, :KV], right[:, KV:]], axis=0)
        r, c = iota((4 * ROWS, 4 * ROWS), 0), iota((4 * ROWS, 4 * ROWS), 1)
        block = r // 48
        quarter = (r - block * 48) // MINE
        item = r - block * 48 - quarter * MINE
        z = (block + lax.axis_index("pz")) & (NZ - 1)
        hot = ones_where(c == quarter * ROWS + z * MINE + item)
        rows = dot(hot, stacked).astype(BF)
        outs = (own, odd_up.at[0], up, odd_up.at[1], None, odd_down.at[1], down, odd_down.at[0])
        for k, out in enumerate(outs):
            if k != 4:
                out[...] = rows[48 * k : 48 * k + 48, :]
        far_up[...] = rows[48 * 4 : 48 * 5, : KV // 2]
        far_down[...] = rows[48 * 4 : 48 * 5, KV // 2 :]

    outs = [array(2, 48, KV)] * 2 + [array(48, KV)] * 3 + [array(48, KV // 2)] * 2
    odd_up, odd_down, own, up, down, far_up, far_down = call(kernel, outs, 300_000_000, 4_000_000)(*terms)
    odd_up = shift(odd_up, "pz", NZ, 1)
    odd_down = shift(odd_down, "pz", NZ, -1)
    far_up = shift(far_up, "pz", NZ, 2)
    far_down = shift(far_down, "pz", NZ, -2)

    def add_kernel(odd_up, odd_down, far_up, far_down, up, down, up_out, down_out):
        half = KV // 2
        for near, odd, far, out, first in ((up, odd_up, far_up, up_out, 0), (down, odd_down, far_down, down_out, half)):
            total = near[...].astype(F32) + odd[1].astype(F32)
            at, rest = slice(first, first + half), slice(half - first, KV - first)
            out[:, at] = (total[:, at] + far[...].astype(F32)).astype(BF)
            out[:, rest] = total[:, rest].astype(BF)

    inputs = (odd_up, odd_down, far_up, far_down, up, down)
    up, down = call(add_kernel, [array(48, KV)] * 2, 1_000_000, 1_000_000)(*inputs)
    up = shift(up, "pz", NZ, 2)
    down = shift(down, "pz", NZ, -2)
    return up, down, odd_up, odd_down, own


def last_sum(parts):
    def kernel(up, down, odd_up, odd_down, own, out):
        total = own[...].astype(F32)
        for term in (odd_up[0], odd_down[0], up[...], down[...]):
            total = total + term.astype(F32)
        for q in range(4):
            out[:, KV * q : KV * q + KV] = total[MINE * q : MINE * q + MINE, :]

    return call(kernel, array(MINE, K, dtype=F32), 1_000_000, 1_000_000)(*parts)


def local(q_fact, p_fact, q_cot, p_cot, passage_of, projection):
    recv = lax.all_to_all(grads(q_fact, p_fact, q_cot, p_cot), ("px", "pz"), 0, 0, tiled=True)
    return last_sum(across_z(across_x(recv, passage_of, permuted(projection))))


def solution(mesh):
    cut = Mesh(mesh.devices.reshape(mesh.shape["pairs"], NX, NZ), ("pairs", "px", "pz"))
    rows = P(("pairs", "px", "pz"), None)
    return jax.shard_map(
        local,
        mesh=cut,
        in_specs=(rows, rows, rows, rows, P("pairs"), P(("px", "pz"), None)),
        out_specs=rows,
        check_vma=False,
    )
```

```python
import jax
import jax.numpy as jnp
from jax import lax
from jax.experimental import pallas as pl
from jax.experimental.pallas import tpu as pltpu
from jax.sharding import Mesh, PartitionSpec as P

KV = 1024
R = 16
QLEN = 32
PLEN = 48
K = 4096
NX, NZ = 4, 8
N = NX * NZ
MINE = 12
PAIRS = N * MINE
G = 1024
ROWS = MINE * 8
MIB = 1024 * 1024
BF = jnp.bfloat16
F32 = jnp.float32
HBM = pl.BlockSpec(memory_space=pltpu.HBM)
WHOLE = pl.BlockSpec(memory_space=pltpu.VMEM)


def iota(shape, dim):
    return lax.broadcasted_iota(jnp.int32, shape, dim)


def dot(a, b):
    return lax.dot_general(a, b, (((1,), (0,)), ((), ())), preferred_element_type=F32)


def ones_where(mask):
    return jnp.where(mask, 1.0, 0.0).astype(BF)


def call(kernel, out_shape, flops, moved, vmem=24, **kwargs):
    return pl.pallas_call(
        kernel,
        out_shape=out_shape,
        compiler_params=pltpu.CompilerParams(vmem_limit_bytes=vmem * MIB),
        cost_estimate=pl.CostEstimate(flops=flops, bytes_accessed=moved, transcendentals=0),
        **kwargs,
    )


def array(*shape, dtype=BF):
    return jax.ShapeDtypeStruct(shape, dtype)


def grads(q_fact, p_fact, q_cot, p_cot):
    steps = 2
    cols = 2 * KV // steps

    def kernel(q_fact, p_fact, q_cot, p_cot, out, q_spread, p_spread):
        step = pl.program_id(0)
        lane = iota((ROWS, 128), 1)
        for kind, (fact, cot, length, spread) in enumerate(
            ((q_fact, q_cot, QLEN, q_spread), (p_fact, p_cot, PLEN, p_spread))
        ):
            tokens = MINE * length

            @pl.when(step % (steps // 2) == 0)
            def _():
                row = iota((2 * ROWS, 2 * R), 0)
                rank = jnp.where(row >= ROWS, 8, 0) + (row & 7) + (step // (steps // 2)) * R
                pick = ones_where(iota((2 * ROWS, 2 * R), 1) == rank)
                row = iota((2 * ROWS, tokens), 0)
                item = jnp.where(row >= ROWS, row - ROWS, row) >> 3
                token = iota((2 * ROWS, tokens), 1) - item * length
                held = (token >= 0) & (token < length)
                spread[...] = jnp.where(held, dot(pick, fact[...]), 0.0).astype(BF)

            grad = dot(spread[...], cot[...])
            for j in range(cols // 128):
                top = grad[:ROWS, 128 * j : 128 * j + 128]
                low = grad[ROWS:, 128 * j : 128 * j + 128]
                at = pl.ds(kind * ROWS, ROWS)
                out[2 * j, at, :] = jnp.where(lane < 64, top, pltpu.roll(low, 64, 1)).astype(BF)
                out[2 * j + 1, at, :] = jnp.where(lane < 64, pltpu.roll(top, 64, 1), low).astype(BF)

    return call(
        kernel,
        array(N, 2 * ROWS, 128),
        800_000_000,
        5_500_000,
        vmem=60,
        grid=(steps,),
        in_specs=[
            pl.BlockSpec((2 * R, MINE * QLEN), lambda n: (0, 0)),
            pl.BlockSpec((2 * R, MINE * PLEN), lambda n: (0, 0)),
            pl.BlockSpec((MINE * QLEN, cols), lambda n: (0, n)),
            pl.BlockSpec((MINE * PLEN, cols), lambda n: (0, n)),
        ],
        out_specs=pl.BlockSpec((N // steps, 2 * ROWS, 128), lambda n: (n, 0, 0)),
        scratch_shapes=[pltpu.VMEM((2 * ROWS, MINE * QLEN), BF), pltpu.VMEM((2 * ROWS, MINE * PLEN), BF)],
    )(q_fact.T, p_fact.T, q_cot, p_cot)


def permuted(projection):
    steps = 4
    cols = K // steps

    def kernel(proj, out, held, made, order, in_sems, out_sems):
        def load(n):
            return pltpu.make_async_copy(proj.at[:, pl.ds(cols * n, cols)], held.at[n], in_sems.at[n])

        def store(n):
            return pltpu.make_async_copy(made.at[n], out.at[n], out_sems.at[n])

        for n in range(steps):
            load(n).start()
        u, v = iota((G, G), 0), iota((G, G), 1)
        order[...] = ones_where(v == (u & 63) * 16 + ((u >> 6) & 1) * 8 + (u >> 7))
        for n in range(steps):
            load(n).wait()
            made[n] = dot(order[...], held[n]).astype(BF)
            store(n).start()
        for n in range(steps):
            store(n).wait()

    return call(
        kernel,
        array(12, G, KV),
        2 * G * G * K,
        16_000_000,
        vmem=57,
        in_specs=[HBM],
        out_specs=HBM,
        scratch_shapes=[
            pltpu.VMEM((steps, G, cols), BF),
            pltpu.VMEM((steps, G, cols), BF),
            pltpu.VMEM((G, G), BF),
            pltpu.SemaphoreType.DMA((steps,)),
            pltpu.SemaphoreType.DMA((steps,)),
        ],
    )(projection)


def rows_of(recv, kind, at, count):
    pieces = []
    while count:
        src, off = at // ROWS, at % ROWS
        take = min(ROWS - off, count)
        pieces.append(recv[src, kind * ROWS + off : kind * ROWS + off + take, :])
        at, count = at + take, count - take
    return jnp.concatenate(pieces, axis=0)


def fetch(proj, held, sems):
    copies = []
    for n in range(4):
        copies.append(pltpu.make_async_copy(proj.at[n], held.at[n], sems.at[n]))
        copies[n].start()
    return copies


def products(pair, copies, held, takes):
    for n in range(4):
        copies[n].wait()
        first, outs = takes[n // 2]
        part = dot(pair[ROWS * first : ROWS * (first + len(outs)), :], held[n]).astype(BF)
        at = KV * (n % 2)
        for d, out in enumerate(outs):
            out[:, at : at + KV] = part[ROWS * d : ROWS * d + ROWS, :]


HELD = [pltpu.VMEM((4, G, KV), BF), pltpu.SemaphoreType.DMA((4,))]


def product_far(recv, passage_of, proj):
    def kernel(recv, passage, proj, pair, l2, r2, wide_q, wide_p, held, sems):
        copies = fetch(proj, held, sems)
        x = lax.axis_index("px")
        r, c = iota((256, 256), 0), iota((256, 256), 1)
        swap = ones_where(c == (r & 31) * 8 + (r >> 5))
        for g in range(PAIRS // 32):
            both = jnp.concatenate([rows_of(recv, kind, 256 * g, 256) for kind in range(2)], axis=1)
            mixed = dot(swap, both).astype(BF)
            for b in range(8):
                wide_q[32 * g : 32 * g + 32, 128 * b : 128 * b + 128] = mixed[32 * b : 32 * b + 32, :128]
                wide_p[32 * g : 32 * g + 32, 128 * b : 128 * b + 128] = mixed[32 * b : 32 * b + 32, 128:]
        hot = ones_where(iota((PAIRS, PAIRS), 0) == passage[...])
        picked = lax.dot_general(hot, wide_p[...], (((0,), (0,)), ((), ())), preferred_element_type=F32)
        summed = (wide_q[...].astype(F32) + picked).astype(BF)
        for i in range(NX):
            at = pl.multiple_of(((i - x) & 3) * ROWS, 32)
            pair[pl.ds(at, ROWS), :] = summed[ROWS * i : ROWS * i + ROWS, :]
        products(pair, copies, held, ((2, (l2,)), (2, (r2,))))

    return call(
        kernel,
        [array(PAIRS, G)] + [array(ROWS, K // 2)] * 2,
        2_000_000_000,
        12_000_000,
        vmem=44,
        in_specs=[WHOLE, WHOLE, HBM],
        scratch_shapes=[pltpu.VMEM((PAIRS, G), BF)] * 2 + HELD,
    )(recv, passage_of.reshape(1, PAIRS), proj)


def product_near(pair, proj):
    def kernel(pair, proj, l3, l0, l1, r3, r0, r1, turned, held, sems):
        copies = fetch(proj, held, sems)
        turned[:ROWS, :] = pair[3 * ROWS :, :]
        turned[ROWS:, :] = pair[: 3 * ROWS, :]
        products(turned, copies, held, ((0, (l3, l0, l1)), (0, (r3, r0, r1))))

    return call(
        kernel,
        [array(ROWS, K // 2)] * 6,
        2_500_000_000,
        10_000_000,
        vmem=44,
        in_specs=[WHOLE, HBM],
        scratch_shapes=[pltpu.VMEM((PAIRS, G), BF)] + HELD,
    )(pair, proj)


def add(a, b):
    return (a.astype(F32) + b.astype(F32)).astype(BF)


def shift(x, axis, size, by):
    return lax.ppermute(x, axis, [(i, (i + by) % size) for i in range(size)])


def across_x(recv, passage_of, proj):
    pair, l2, r2 = product_far(recv, passage_of, proj)
    far_l = shift(l2, "px", NX, 1)
    far_r = shift(r2, "px", NX, -1)
    l3, l0, l1, r3, r0, r1 = product_near(pair, proj)
    got_l = shift(l3, "px", NX, -1)
    got_r = shift(r1, "px", NX, 1)
    far_l, far_r = lax.optimization_barrier((far_l, far_r))
    sum_l = shift(add(l1, far_l), "px", NX, 1)
    sum_r = shift(add(r3, far_r), "px", NX, -1)
    return sum_l, sum_r, got_l, got_r, l0, r0


def across_z(terms):
    def kernel(l2, r2, l1, r1, l0, r0, odd_up, odd_down, own, up, down, far_up, far_down):
        left = (l0[...].astype(F32) + l1[...].astype(F32) + l2[...].astype(F32)).astype(BF)
        right = (r0[...].astype(F32) + r1[...].astype(F32) + r2[...].astype(F32)).astype(BF)
        stacked = jnp.concatenate([left[:, :KV], left[:, KV:], right[:, :KV], right[:, KV:]], axis=0)
        r, c = iota((4 * ROWS, 4 * ROWS), 0), iota((4 * ROWS, 4 * ROWS), 1)
        block = r // 48
        quarter = (r - block * 48) // MINE
        item = r - block * 48 - quarter * MINE
        z = (block + lax.axis_index("pz")) & (NZ - 1)
        hot = ones_where(c == quarter * ROWS + z * MINE + item)
        rows = dot(hot, stacked).astype(BF)
        outs = (own, odd_up.at[0], up, odd_up.at[1], None, odd_down.at[1], down, odd_down.at[0])
        for k, out in enumerate(outs):
            if k != 4:
                out[...] = rows[48 * k : 48 * k + 48, :]
        far_up[...] = rows[48 * 4 : 48 * 5, : KV // 2]
        far_down[...] = rows[48 * 4 : 48 * 5, KV // 2 :]

    outs = [array(2, 48, KV)] * 2 + [array(48, KV)] * 3 + [array(48, KV // 2)] * 2
    odd_up, odd_down, own, up, down, far_up, far_down = call(kernel, outs, 300_000_000, 4_000_000)(*terms)
    odd_up = shift(odd_up, "pz", NZ, 1)
    odd_down = shift(odd_down, "pz", NZ, -1)
    far_up = shift(far_up, "pz", NZ, 2)
    far_down = shift(far_down, "pz", NZ, -2)

    def add_kernel(odd_up, odd_down, far_up, far_down, up, down, up_out, down_out):
        half = KV // 2
        for near, odd, far, out, first in ((up, odd_up, far_up, up_out, 0), (down, odd_down, far_down, down_out, half)):
            total = near[...].astype(F32) + odd[1].astype(F32)
            at, rest = slice(first, first + half), slice(half - first, KV - first)
            out[:, at] = (total[:, at] + far[...].astype(F32)).astype(BF)
            out[:, rest] = total[:, rest].astype(BF)

    inputs = (odd_up, odd_down, far_up, far_down, up, down)
    up, down = call(add_kernel, [array(48, KV)] * 2, 1_000_000, 1_000_000)(*inputs)
    up = shift(up, "pz", NZ, 2)
    down = shift(down, "pz", NZ, -2)
    return up, down, odd_up, odd_down, own


def last_sum(parts):
    def kernel(up, down, odd_up, odd_down, own, out):
        total = own[...].astype(F32)
        for term in (odd_up[0], odd_down[0], up[...], down[...]):
            total = total + term.astype(F32)
        for q in range(4):
            out[:, KV * q : KV * q + KV] = total[MINE * q : MINE * q + MINE, :]

    return call(kernel, array(MINE, K, dtype=F32), 1_000_000, 1_000_000)(*parts)


def local(q_fact, p_fact, q_cot, p_cot, passage_of, projection):
    recv = lax.all_to_all(grads(q_fact, p_fact, q_cot, p_cot), ("px", "pz"), 0, 0, tiled=True)
    return last_sum(across_z(across_x(recv, passage_of, permuted(projection))))


def solution(mesh):
    cut = Mesh(mesh.devices.reshape(mesh.shape["pairs"], NX, NZ), ("pairs", "px", "pz"))
    rows = P(("pairs", "px", "pz"), None)
    return jax.shard_map(
        local,
        mesh=cut,
        in_specs=(rows, rows, rows, rows, P("pairs"), P(("px", "pz"), None)),
        out_specs=rows,
        check_vma=False,
    )
```
